128 devices in a mesh: slab: 16 (over z, x_lo, core), head: 8 (over x_hi, y).
Axes of the slice: x: 4 (x_hi: 2, x_lo: 2; x = x_hi * 2 + x_lo), y: 4, z: 4, core: 2. Of those that a mesh axis runs over, the one named last changes fastest.
Arguments:
- hidden: bfloat16 [12288, 3072], P('slab', 'head'), may hold values from -48 to 48
- w_qkv: bfloat16 [3072, 3, 3072], P(None, None, 'head'), may hold values from -0.109375 to 0.109375
- text_keys: bfloat16 [2, 256, 3072], P(None, None, 'head'), may hold values from -6 to 6
- text_values: bfloat16 [2, 256, 3072], P(None, None, 'head'), may hold values from -6 to 6
- text_len: int32 [2], replicated, may hold values from 64 to 256, as said below
- advantage: float32 [2], replicated, may hold values from -2 to 2
- out_grad: bfloat16 [12288, 3072], P('slab', 'head'), may hold values from -6 to 6
- tile_lists: int32 [32, 3], P('slab'), may hold values from -1 to 31, as said below
Outputs:
- hidden_grad: bfloat16 [12288, 3072], P('slab', 'head')
- weight_grad: bfloat16 [3072, 3, 3072], P('slab', None, 'head')
- text_grad: bfloat16 [2, 256, 2, 3072], P(None, None, None, 'head')
The draws below stay inside these ranges and needn't reach their ends.
Inputs may be any that keep to these rules, and one draw needn't show every extreme that they name: `tile_lists`: tiles lie on a grid of (16) time layers by 2 samples by 1 tiles, numbered time, sample, width from slowest. Row i lists, in random order, itself, every tile of the same sample and time layer within one step in width, and some of the tiles of the same sample within one step in time and width, followed by -1 in the remaining slots; j is in row i exactly when i is in row j. `text_len`: some sample has all 256 text tokens live.
All inputs are finite; a program needn't handle non-finite values.
Results may differ from the reference program's by a relative error of at most 0.014.
The reference program's roundings to bfloat16 on the way count: a program that leaves them out, or rounds other values in their place, can miss the bound.
Values may be sent and summed in bfloat16 or wider, within the bound.
No kernel may reach another device: no remote copies, remote signals or barrier semaphores. Data moves between devices by JAX's collectives and lax.ppermute only.
A program may use at most 128 MiB of HBM per device.

```python
import math
import jax
import jax.numpy as jnp
from jax import lax

D = 3072
HEADS = 24
DH = 128
TILE = 384
GW = 1
SAMPLES = 2
TEXT = 256
NB = 3
TILES_DEV = 2
TILES = 32
TOKENS = 12288


def draw_hidden(key, part):
    key = jax.random.fold_in(key, 11)
    base_key, row_key = jax.random.split(key)
    base = jax.random.normal(base_key, (TOKENS, D), jnp.float32)
    row_scale = jnp.exp(jax.random.uniform(row_key, (TOKENS, 1), jnp.float32, math.log(0.5), math.log(2.0)))
    return jnp.clip(base * row_scale, -48.0, 48.0).astype(jnp.bfloat16)


def draw_text_len(key, part):
    key = jax.random.fold_in(key, 23)
    len_key, pick_key = jax.random.split(key)
    counts = jax.random.randint(len_key, (SAMPLES,), TEXT // 4, TEXT + 1)
    chosen = jax.random.randint(pick_key, (), 0, SAMPLES)
    return jnp.where(jnp.arange(SAMPLES) == chosen, TEXT, counts).astype(jnp.int32)


def draw_advantage(key, part):
    key = jax.random.fold_in(key, 37)
    size_key, sign_key = jax.random.split(key)
    magnitude = jnp.exp(jax.random.uniform(size_key, (SAMPLES,), jnp.float32, math.log(0.5), math.log(2.0)))
    signs = jnp.where(jax.random.bernoulli(sign_key, 0.5, (SAMPLES,)), 1.0, -1.0)
    return (magnitude * signs).astype(jnp.float32)


def draw_tile_lists(key, part):
    key = jax.random.fold_in(key, 5)
    bit_key, pick_key, order_key = jax.random.split(key, 3)
    layers = TILES // TILES_DEV
    tile = jnp.arange(TILES, dtype=jnp.int32)
    layer = tile // TILES_DEV
    sample = tile % TILES_DEV // GW
    column = tile % GW
    offset = jnp.arange(9, dtype=jnp.int32)
    step_t = offset // 3 - 1
    step_w = offset % 3 - 1
    new_t = layer[:, None] + step_t[None, :]
    new_w = column[:, None] + step_w[None, :]
    inside = (new_t >= 0) & (new_t < layers) & (new_w >= 0) & (new_w < GW)
    named = new_t * TILES_DEV + sample[:, None] * GW + new_w
    bits = jax.random.randint(bit_key, (layers, SAMPLES, GW, 3), 0, 2)
    chosen = jax.random.randint(pick_key, (layers,), 0, SAMPLES)
    upward = step_t[None, :] > 0
    low_t = jnp.clip(jnp.where(upward, layer[:, None], layer[:, None] - 1), 0, layers - 1)
    low_w = jnp.clip(jnp.where(upward, column[:, None], new_w), 0, GW - 1)
    low_d = jnp.where(upward, step_w[None, :], -step_w[None, :]) + 1
    sample_b = jnp.broadcast_to(sample[:, None], low_t.shape)
    bit = bits[low_t, sample_b, low_w, low_d]
    kept_cross = (chosen[low_t] != sample_b) | (bit == 1)
    keep = inside & ((step_t[None, :] == 0) | kept_cross)
    priority = jax.random.randint(order_key, (TILES, 9), 0, 1024) * 16 + offset[None, :]
    score = jnp.where(keep, priority, 100000 + offset[None, :])
    order = jnp.argsort(score, axis=1)[:, :NB]
    picked = jnp.take_along_axis(jnp.where(keep, named, -1), order, axis=1)
    return picked.astype(jnp.int32)


def levels(stream_key, shape, cuts, low, high):
    def one(position, shards_of):
        draws = jax.random.uniform(jax.random.fold_in(jax.random.fold_in(stream_key, 6), position), (shards_of,), jnp.float32, low / len(cuts), high / len(cuts))
        return jnp.repeat(jnp.exp(draws), shape[position] // shards_of).reshape((-1,) + (1,) * (len(shape) - position - 1))

    level = one(*cuts[0])
    for cut in cuts[1:]:
        level = level * one(*cut)
    return level


def gaussian(key, extent, scale, limit, shards=(), held_as=jnp.bfloat16):
    array = jax.random.normal(key, extent, jnp.float32) * scale
    if len(shards) > 0:
        array = levels(key, extent, shards, -0.22, 0.18) * array
    return jnp.clip(array, min=-limit, max=limit).astype(held_as)


def setup_inputs(seed: int = 0) -> dict:
    key_of = jax.random.split(jax.random.key(seed), 9)
    hidden = draw_hidden(jax.random.fold_in(key_of[8], 71), 0)
    w_qkv = gaussian(key_of[1], (D, 3, HEADS * DH), D ** -0.5, 0.109375, ((2, 8),))
    text_keys = gaussian(key_of[2], (SAMPLES, TEXT, HEADS * DH), 1.0, 6.0, ((2, 8),))
    text_values = gaussian(key_of[3], (SAMPLES, TEXT, HEADS * DH), 1.0, 6.0, ((2, 8),))
    text_len = draw_text_len(jax.random.fold_in(key_of[8], 71), 0)
    advantage = draw_advantage(jax.random.fold_in(key_of[8], 71), 0)
    out_grad = gaussian(key_of[6], (TOKENS, HEADS * DH), 1.0, 6.0, ((0, 16), (1, 8)))
    tile_lists = draw_tile_lists(jax.random.fold_in(key_of[8], 71), 0)
    return dict(hidden=hidden, w_qkv=w_qkv, text_keys=text_keys, text_values=text_values, text_len=text_len, advantage=advantage, out_grad=out_grad, tile_lists=tile_lists)


def reference(hidden, w_qkv, text_keys, text_values, text_len, advantage, out_grad, tile_lists):
    f32 = jnp.float32
    bf16 = jnp.bfloat16
    scale = 1.0 / math.sqrt(DH)
    proj = jnp.einsum('td,dch->tch', hidden.astype(f32), w_qkv.astype(f32)).astype(bf16)
    group = TILES_DEV // SAMPLES
    tile_sample = jnp.arange(TILES, dtype=jnp.int32) % TILES_DEV // group
    adv_rows = jnp.repeat(advantage[tile_sample], TILE)
    out_cot = (adv_rows[:, None] * out_grad.astype(f32)).astype(bf16)
    q_tiles = proj[:, 0].reshape(TILES, TILE, HEADS, DH)
    k_tiles = proj[:, 1].reshape(TILES, TILE, HEADS, DH)
    v_tiles = proj[:, 2].reshape(TILES, TILE, HEADS, DH)
    o_tiles = out_cot.reshape(TILES, TILE, HEADS, DH)
    text_k = text_keys.reshape(SAMPLES, TEXT, HEADS, DH)
    text_v = text_values.reshape(SAMPLES, TEXT, HEADS, DH)
    nvid = NB * TILE

    def step(carry, index):
        dk_acc, dv_acc, tk_acc, tv_acc = carry
        listed = tile_lists[index]
        usable = listed >= 0
        slots = jnp.where(usable, listed, 0).astype(jnp.int32)
        sample = (index % TILES_DEV // group).astype(jnp.int32)
        keys = jnp.concatenate([k_tiles[slots].reshape(nvid, HEADS, DH), text_k[sample]], 0).astype(f32)
        vals = jnp.concatenate([v_tiles[slots].reshape(nvid, HEADS, DH), text_v[sample]], 0).astype(f32)
        key_mask = jnp.concatenate([jnp.repeat(usable, TILE), jnp.arange(TEXT, dtype=jnp.int32) < text_len[sample]])
        query = q_tiles[index].astype(f32)
        cot = o_tiles[index].astype(f32)
        scores = jnp.einsum('qhd,khd->hqk', query, keys) * scale
        scores = jnp.where(key_mask[None, None, :], scores, -jnp.inf)
        top = lax.optimization_barrier(jnp.max(scores, axis=2, keepdims=True))
        lse = top + jnp.log(lax.optimization_barrier(jnp.sum(jnp.exp(scores - top), axis=2, keepdims=True)))
        probs = jnp.exp(scores - lse)
        probs_b = probs.astype(bf16).astype(f32)
        attn = jnp.einsum('hqk,khd->qhd', probs_b, vals)
        delta = lax.optimization_barrier(jnp.sum(cot * attn, axis=2))
        dprobs = jnp.einsum('qhd,khd->hqk', cot, vals)
        dscores = (probs * (dprobs - delta.T[:, :, None]) * scale).astype(bf16).astype(f32)
        query_grad = jnp.einsum('hqk,khd->qhd', dscores, keys)
        key_part = jnp.einsum('hqk,qhd->khd', dscores, query)
        value_part = jnp.einsum('hqk,qhd->khd', probs_b, cot)
        dk_acc = dk_acc.at[slots].add(key_part[:nvid].reshape(NB, TILE, HEADS, DH))
        dv_acc = dv_acc.at[slots].add(value_part[:nvid].reshape(NB, TILE, HEADS, DH))
        tk_acc = tk_acc.at[sample].add(key_part[nvid:])
        tv_acc = tv_acc.at[sample].add(value_part[nvid:])
        return ((dk_acc, dv_acc, tk_acc, tv_acc), query_grad.astype(bf16))
    init = (jnp.zeros((TILES, TILE, HEADS, DH), f32), jnp.zeros((TILES, TILE, HEADS, DH), f32), jnp.zeros((SAMPLES, TEXT, HEADS, DH), f32), jnp.zeros((SAMPLES, TEXT, HEADS, DH), f32))
    sums, query_grads = lax.scan(step, init, jnp.arange(TILES, dtype=jnp.int32))
    dk_acc, dv_acc, tk_acc, tv_acc = sums
    width = HEADS * DH
    grads = jnp.stack([query_grads.reshape(TOKENS, width), dk_acc.reshape(TOKENS, width).astype(bf16), dv_acc.reshape(TOKENS, width).astype(bf16)], axis=1)
    text_grad = jnp.stack([tk_acc.reshape(SAMPLES, TEXT, width), tv_acc.reshape(SAMPLES, TEXT, width)], axis=2).astype(bf16)
    hidden_grad = jnp.einsum('tch,dch->td', grads.astype(f32), w_qkv.astype(f32)).astype(bf16)
    weight_grad = jnp.einsum('td,tch->dch', hidden.astype(f32), grads.astype(f32)).astype(bf16)
    return (hidden_grad, weight_grad, text_grad)
```

```python
import math

import jax
import jax.numpy as jnp
from jax import lax
from jax.experimental import pallas as pl
from jax.experimental.pallas import tpu as pltpu
from jax.sharding import PartitionSpec as P

DH = 128
TILE = 384
SAMPLES = 2
HEADS_DEV = 3
CH = 384
TEXT = 256
BF = jnp.bfloat16
F32 = jnp.float32
SCALE = 1.0 / math.sqrt(DH)
EXP_SCALE = SCALE * math.log2(math.e)
MIB = 1024 * 1024

VMEM = pl.BlockSpec(memory_space=pltpu.VMEM)
SMEM = pl.BlockSpec(memory_space=pltpu.SMEM)


def dot(a, b, ca, cb):
    return lax.dot_general(a, b, (((ca,), (cb,)), ((), ())), preferred_element_type=F32)


def head_move(x, dx, dy):
    pairs = [(h, ((h // 4) ^ dx) * 4 + (h + dy) % 4) for h in range(8)]
    return lax.ppermute(x, "head", pairs)


def slab_move(x, dz, dx, dc):
    pairs = [
        (s, ((s // 4 + dz) % 4) * 4 + ((s // 2 % 2) ^ dx) * 2 + ((s % 2) ^ dc)) for s in range(16)
    ]
    return lax.ppermute(x, "slab", pairs)


def slab_step(x, distance):
    pairs = [(i, i + distance) for i in range(16) if 0 <= i + distance < 16]
    return lax.ppermute(x, "slab", pairs)


PAIRS = ((0, 0, 1), (3, 2, 4), (1, 3, 5), (2, 6, 7))


def project_kernel(meta, *refs):
    chunks, (w, q_out, kv_out, mine, other, acc) = (refs[:8], refs[8:])
    a, y, core = (meta[0], meta[1], meta[2])
    for n, (d, r0, r1) in enumerate(PAIRS):
        yj = (y + d) & 3
        pair = ((a * 4 + yj, chunks[r0]), ((1 - a) * 4 + yj, chunks[r1]))
        x = jnp.concatenate([pair[0][1][...], pair[1][1][...]], axis=1)
        for c in range(3):
            wc = jnp.concatenate([w[c, pair[0][0]], w[c, pair[1][0]]], axis=0)
            part = dot(x, wc, 1, 0)
            if n == 0:
                acc[c] = part
            else:
                acc[c] += part
        own = ((yj ^ core) & 1) == 0
        for j, ref in pair:
            z = j >> 1

            @pl.when(own)
            def _():
                mine[z] = ref[...]

            @pl.when(jnp.logical_not(own))
            def _():
                other[z] = ref[...]

    q_out[...] = acc[0].astype(BF)
    for h in range(HEADS_DEV):
        cols = slice(h * DH, (h + 1) * DH)
        kv_out[:, 2 * h * DH : (2 * h + 1) * DH] = acc[1, :, cols].astype(BF)
        kv_out[:, (2 * h + 1) * DH : (2 * h + 2) * DH] = acc[2, :, cols].astype(BF)


def project(meta, chunks, w):
    return pl.pallas_call(
        project_kernel,
        in_specs=[SMEM] + [VMEM] * 9,
        out_specs=[VMEM] * 4,
        out_shape=[
            jax.ShapeDtypeStruct((TILE, CH), BF),
            jax.ShapeDtypeStruct((TILE, 2 * CH), BF),
            jax.ShapeDtypeStruct((4, TILE, CH), BF),
            jax.ShapeDtypeStruct((4, TILE, CH), BF),
        ],
        scratch_shapes=[pltpu.VMEM((3, TILE, CH), F32)],
        compiler_params=pltpu.CompilerParams(vmem_limit_bytes=40 * MIB),
        cost_estimate=pl.CostEstimate(
            flops=2 * TILE * 3072 * 1152, bytes_accessed=14 * MIB, transcendentals=0
        ),
        name="project",
    )(meta, *chunks, w)


def attention_kernel(
    meta, adv, q_ref, prev, own, nxt, tk_ref, tv_ref, og_ref, dq, dprev, down, dnext, dtext
):
    q = q_ref[...]
    cot = (adv[0] * og_ref[...].astype(F32)).astype(BF)
    rows = lax.broadcasted_iota(jnp.int32, (TEXT, TILE), 0)
    live = rows < meta[2]
    keys = [prev[:, :DH], own[:, :DH], nxt[:, :DH], tk_ref[0]]
    vals = [prev[:, DH:], own[:, DH:], nxt[:, DH:], tv_ref[0]]
    scores = [dot(k, q, 1, 1) for k in keys]
    scores[0] = jnp.where(meta[0] > 0, scores[0], -jnp.inf)
    scores[2] = jnp.where(meta[1] > 0, scores[2], -jnp.inf)
    scores[3] = jnp.where(live, scores[3], -jnp.inf)
    top = jnp.max(scores[1], axis=0, keepdims=True)
    for n in (0, 2, 3):
        top = jnp.maximum(top, jnp.max(scores[n], axis=0, keepdims=True))
    powers = [jnp.exp2((s - top) * EXP_SCALE) for s in scores]
    total = sum(jnp.sum(p, axis=0, keepdims=True) for p in powers)
    inverse = 1.0 / total
    probs = [p * inverse for p in powers]
    probs_b = [p.astype(BF) for p in probs]
    dprobs = [dot(v, cot, 1, 1) for v in vals]
    delta = sum(
        jnp.sum(p.astype(F32) * d, axis=0, keepdims=True) for p, d in zip(probs_b, dprobs)
    )
    dscores = [(p * (d - delta) * SCALE).astype(BF) for p, d in zip(probs, dprobs)]
    grad = dot(keys[0], dscores[0], 0, 0)
    for n in (1, 2, 3):
        grad += dot(keys[n], dscores[n], 0, 0)
    dq[...] = grad.T.astype(BF)
    for n, out in ((0, dprev), (1, down), (2, dnext)):
        out[:, :DH] = dot(dscores[n], q, 1, 0).astype(out.dtype)
        out[:, DH:] = dot(probs_b[n], cot, 1, 0).astype(out.dtype)
    dtext[0] = dot(dscores[3], q, 1, 0).astype(BF)
    dtext[1] = dot(probs_b[3], cot, 1, 0).astype(BF)


def attention(sample, meta, adv, q, prev, own, nxt, text_k, text_v, out_grad):
    kv = pl.BlockSpec((TILE, 2 * DH), lambda h: (0, h))
    tile = pl.BlockSpec((TILE, DH), lambda h: (0, h))
    text = pl.BlockSpec((1, TEXT, DH), lambda h: (sample, 0, h))
    return pl.pallas_call(
        attention_kernel,
        grid=(HEADS_DEV,),
        in_specs=[
            SMEM,
            SMEM,
            tile,
            kv,
            kv,
            kv,
            text,
            text,
            pl.BlockSpec((TILE, DH), lambda h: (sample, h)),
        ],
        out_specs=[tile, kv, kv, kv, pl.BlockSpec((2, TEXT, DH), lambda h: (0, 0, h))],
        out_shape=[
            jax.ShapeDtypeStruct((TILE, CH), BF),
            jax.ShapeDtypeStruct((TILE, 2 * CH), BF),
            jax.ShapeDtypeStruct((TILE, 2 * CH), F32),
            jax.ShapeDtypeStruct((TILE, 2 * CH), BF),
            jax.ShapeDtypeStruct((2, TEXT, CH), BF),
        ],
        compiler_params=pltpu.CompilerParams(vmem_limit_bytes=40 * MIB),
        cost_estimate=pl.CostEstimate(
            flops=20 * 3 * 384 * 1408 * 128, bytes_accessed=8 * MIB, transcendentals=3 * 384 * 1408
        ),
        name="attention",
    )(meta, adv, q, prev, own, nxt, text_k, text_v, out_grad)


def hidden_kernel(meta, dq, down, low, high, w, grads, *outs):
    a, y = (meta[0], meta[1])
    kv = down[...] + low[...].astype(F32) + high[...].astype(F32)
    grads[:, :CH] = dq[...]
    for h in range(HEADS_DEV):
        cols = slice(h * DH, (h + 1) * DH)
        grads[:, CH + h * DH : CH + (h + 1) * DH] = kv[:, 2 * h * DH : (2 * h + 1) * DH].astype(BF)
        grads[:, 2 * CH + h * DH : 2 * CH + (h + 1) * DH] = kv[
            :, (2 * h + 1) * DH : (2 * h + 2) * DH
        ].astype(BF)
    for d in (2, 1, 3, 0):
        yj = (y + d) & 3
        j0, j1 = (a * 4 + yj, (1 - a) * 4 + yj)
        part = None
        for c in range(3):
            wc = jnp.concatenate([w[c, j0], w[c, j1]], axis=0)
            term = dot(grads[:, c * CH : (c + 1) * CH], wc, 1, 1)
            part = term if part is None else part + term
        outs[d][...] = part[:, :CH].astype(BF)
        outs[4 + d][...] = part[:, CH:].astype(BF)


def hidden_parts(meta, dq, down, low, high, w):
    shape = jax.ShapeDtypeStruct((TILE, CH), BF)
    return pl.pallas_call(
        hidden_kernel,
        in_specs=[SMEM] + [VMEM] * 5,
        out_specs=[VMEM] * 9,
        out_shape=[jax.ShapeDtypeStruct((TILE, 3 * CH), BF)] + [shape] * 8,
        compiler_params=pltpu.CompilerParams(vmem_limit_bytes=40 * MIB),
        cost_estimate=pl.CostEstimate(
            flops=2 * TILE * 3072 * 1152, bytes_accessed=14 * MIB, transcendentals=0
        ),
        name="hidden_parts",
    )(meta, dq, down, low, high, w)


def add(*terms):
    total = terms[0].astype(F32)
    for term in terms[1:]:
        total = total + term.astype(F32)
    return total.astype(BF)


def hidden_reduce(parts):
    same, flip = (parts[:4], parts[4:])
    far_flip = head_move(flip[2], 0, 1)
    far_same = head_move(same[2], 0, 3)
    flip_up = head_move(add(flip[1], far_flip), 0, 1)
    flip_down = head_move(flip[3], 0, 3)
    same_down = head_move(add(same[3], far_same), 0, 3)
    same_up = head_move(same[1], 0, 1)
    across = head_move(add(flip[0], flip_up, flip_down), 1, 0)
    return add(same[0], same_up, same_down, across)


def weight_kernel(meta, x0, x1, p0, p1, g0, g1, h0, h1, *outs):
    z = meta[3]
    g = jnp.concatenate([g0[...], g1[...], h0[...], h1[...]], axis=0)
    for d in (2, 1, 3, 0):
        j = (z + d) & 3
        x = jnp.concatenate([x0[j], x1[j], p0[j], p1[j]], axis=0)
        outs[d][...] = dot(x, g, 0, 0).astype(BF)


def weight_parts(meta, *arrays):
    shape = jax.ShapeDtypeStruct((CH, 3 * CH), BF)
    return pl.pallas_call(
        weight_kernel,
        in_specs=[SMEM] + [VMEM] * 8,
        out_specs=[VMEM] * 4,
        out_shape=[shape] * 4,
        compiler_params=pltpu.CompilerParams(vmem_limit_bytes=48 * MIB),
        cost_estimate=pl.CostEstimate(
            flops=2 * 768 * 3072 * 1152, bytes_accessed=16 * MIB, transcendentals=0
        ),
        name="weight_parts",
    )(meta, *arrays)


def weight_reduce(parts, x_lo, core):
    got = [slab_move(parts[d], d, 0, 0) for d in (2, 1, 3)]
    total = add(parts[0], *got)
    halves = total.reshape(2, CH // 2, 3 * CH)
    home = x_lo == core
    near = lax.dynamic_index_in_dim(halves, jnp.where(home, 1 - core, core), 0, keepdims=False)
    far = lax.dynamic_index_in_dim(halves, jnp.where(home, core, 1 - core), 0, keepdims=False)
    first, second = ([], [])
    for s in range(16):
        z, x, c = (s // 4, s // 2 % 2, s % 2)
        if x == c:
            first.append((s, z * 4 + x * 2 + 1 - c))
        else:
            first.append((s, z * 4 + (1 - x) * 2 + c))
            second.append((s, z * 4 + (1 - x) * 2 + 1 - c))
    got_first = lax.ppermute(near, "slab", first)
    got_second = lax.ppermute(far, "slab", second)
    return add(jnp.where(home, far, got_second), got_first)


def text_reduce(terms, core):
    both = jnp.stack(terms, axis=1).reshape(2, SAMPLES * TEXT, CH)
    keep = lax.dynamic_index_in_dim(both, core, 0, keepdims=False)
    give = lax.dynamic_index_in_dim(both, 1 - core, 0, keepdims=False)
    part = add(keep, slab_move(give, 0, 0, 1)).reshape(4, -1, CH)
    z = lax.axis_index("slab") // 4

    def at(d):
        return lax.dynamic_index_in_dim(part, (z + d) % 4, 0, keepdims=False)

    quarter = add(at(0), *[slab_move(at(d), d, 0, 0) for d in (2, 1, 3)])
    quarter = add(quarter, slab_move(quarter, 0, 1, 0))
    full = jnp.zeros_like(part)
    full = lax.dynamic_update_index_in_dim(full, quarter, z, 0)
    for d in (2, 1, 3):
        full = lax.dynamic_update_index_in_dim(full, slab_move(quarter, d, 0, 0), (z - d) % 4, 0)
    full = full.reshape(SAMPLES, TEXT, CH)
    twin = slab_move(full, 0, 0, 1)
    key = jnp.where(core == 0, full, twin)
    value = jnp.where(core == 0, twin, full)
    return jnp.stack([key, value], axis=2)


def gather_chunks(own):
    flip = head_move(own, 1, 0)
    below = head_move(own, 0, 1)
    above = head_move(own, 0, 3)
    flip_below = head_move(flip, 0, 1)
    flip_above = head_move(flip, 0, 3)
    far = head_move(below, 0, 1)
    far_flip = head_move(flip_above, 0, 3)
    return [own, flip, below, above, flip_below, flip_above, far, far_flip]


def body(hidden, w_qkv, text_keys, text_values, text_len, advantage, out_grad, tile_lists):
    slab = lax.axis_index("slab")
    head = lax.axis_index("head")
    core = slab % 2
    x_lo = slab // 2 % 2
    place = jnp.stack([head // 4, head % 4, core, slab // 4]).astype(jnp.int32)
    w = jnp.transpose(w_qkv, (1, 0, 2)).reshape(3, 8, CH, CH)
    index = jnp.arange(SAMPLES, dtype=jnp.int32)[:, None] + slab * SAMPLES
    has_prev = jnp.any((tile_lists == index - SAMPLES) & (tile_lists >= 0), axis=1)
    has_next = jnp.any(tile_lists == index + SAMPLES, axis=1)
    flags = jnp.stack(
        [has_prev.astype(jnp.int32), has_next.astype(jnp.int32), text_len], axis=1
    )
    dqs, grads, mines, theirs, texts, hidden_grads = ([], [], [], [], [], [])
    for s in range(SAMPLES):
        chunks = gather_chunks(hidden[s * TILE : (s + 1) * TILE])
        q, kv, mine, other = project(place, chunks, w)
        mines.append(mine)
        theirs.append(slab_move(other, 0, 0, 1))
        prev = slab_step(kv, 1)
        nxt = slab_step(kv, -1)
        dq, dprev, down, dnext, dtext = attention(
            s, flags[s], advantage[s : s + 1], q, prev, kv, nxt, text_keys, text_values, out_grad
        )
        texts.append(dtext)
        low = slab_step(dnext, 1)
        high = slab_step(dprev, -1)
        made = hidden_parts(place, dq, down, low, high, w)
        grads.append(made[0])
        hidden_grads.append(hidden_reduce(made[1:]))
    twins = [slab_move(g, 0, 0, 1) for g in grads]
    parts = weight_parts(place, *mines, *theirs, *grads, *twins)
    weight_grad = weight_reduce(parts, x_lo, core).reshape(CH // 2, 3, CH)
    text_grad = text_reduce(texts, core)
    hidden_grad = jnp.concatenate(hidden_grads, axis=0)
    return (hidden_grad, weight_grad, text_grad)


def solution(mesh):
    in_specs = (
        P("slab", "head"),
        P(None, None, "head"),
        P(None, None, "head"),
        P(None, None, "head"),
        P(),
        P(),
        P("slab", "head"),
        P("slab", None),
    )
    out_specs = (P("slab", "head"), P("slab", None, "head"), P(None, None, None, "head"))
    return jax.shard_map(body, mesh=mesh, in_specs=in_specs, out_specs=out_specs, check_vma=False)
```

```python
import math

import jax
import jax.numpy as jnp
from jax import lax
from jax.experimental import pallas as pl
from jax.experimental.pallas import tpu as pltpu
from jax.sharding import PartitionSpec as P

DH = 128
TILE = 384
SAMPLES = 2
HEADS_DEV = 3
CH = 384
TEXT = 256
BF = jnp.bfloat16
F32 = jnp.float32
SCALE = 1.0 / math.sqrt(DH)
EXP_SCALE = SCALE * math.log2(math.e)
MIB = 1024 * 1024

VMEM = pl.BlockSpec(memory_space=pltpu.VMEM)
SMEM = pl.BlockSpec(memory_space=pltpu.SMEM)


def dot(a, b, ca, cb):
    return lax.dot_general(a, b, (((ca,), (cb,)), ((), ())), preferred_element_type=F32)


def head_move(x, dx, dy):
    pairs = [(h, ((h // 4) ^ dx) * 4 + (h + dy) % 4) for h in range(8)]
    return lax.ppermute(x, "head", pairs)


def slab_move(x, dz, dx, dc):
    pairs = [
        (s, ((s // 4 + dz) % 4) * 4 + ((s // 2 % 2) ^ dx) * 2 + ((s % 2) ^ dc)) for s in range(16)
    ]
    return lax.ppermute(x, "slab", pairs)


def slab_step(x, distance):
    pairs = [(i, i + distance) for i in range(16) if 0 <= i + distance < 16]
    return lax.ppermute(x, "slab", pairs)


PAIRS = ((0, 0, 1), (3, 2, 4), (1, 3, 5), (2, 6, 7))


def project_kernel(meta, *refs):
    chunks, (w, q_out, kv_out, mine, other, acc) = (refs[:8], refs[8:])
    a, y, core = (meta[0], meta[1], meta[2])
    for n, (d, r0, r1) in enumerate(PAIRS):
        yj = (y + d) & 3
        pair = ((a * 4 + yj, chunks[r0]), ((1 - a) * 4 + yj, chunks[r1]))
        x = jnp.concatenate([pair[0][1][...], pair[1][1][...]], axis=1)
        for c in range(3):
            wc = jnp.concatenate([w[c, pair[0][0]], w[c, pair[1][0]]], axis=0)
            part = dot(x, wc, 1, 0)
            if n == 0:
                acc[c] = part
            else:
                acc[c] += part
        own = ((yj ^ core) & 1) == 0
        for j, ref in pair:
            z = j >> 1

            @pl.when(own)
            def _():
                mine[z] = ref[...]

            @pl.when(jnp.logical_not(own))
            def _():
                other[z] = ref[...]

    q_out[...] = acc[0].astype(BF)
    for h in range(HEADS_DEV):
        cols = slice(h * DH, (h + 1) * DH)
        kv_out[:, 2 * h * DH : (2 * h + 1) * DH] = acc[1, :, cols].astype(BF)
        kv_out[:, (2 * h + 1) * DH : (2 * h + 2) * DH] = acc[2, :, cols].astype(BF)


def project(meta, chunks, w):
    return pl.pallas_call(
        project_kernel,
        in_specs=[SMEM] + [VMEM] * 9,
        out_specs=[VMEM] * 4,
        out_shape=[
            jax.ShapeDtypeStruct((TILE, CH), BF),
            jax.ShapeDtypeStruct((TILE, 2 * CH), BF),
            jax.ShapeDtypeStruct((4, TILE, CH), BF),
            jax.ShapeDtypeStruct((4, TILE, CH), BF),
        ],
        scratch_shapes=[pltpu.VMEM((3, TILE, CH), F32)],
        compiler_params=pltpu.CompilerParams(vmem_limit_bytes=16 * MIB),
        cost_estimate=pl.CostEstimate(
            flops=2 * TILE * 3072 * 1152, bytes_accessed=14 * MIB, transcendentals=0
        ),
        name="project",
    )(meta, *chunks, w)


def attention_kernel(
    meta, adv, q_ref, prev, own, nxt, tk_ref, tv_ref, og_ref, swap, dprev, down, dnext, keep
):
    q = q_ref[...]
    cot = (adv[0] * og_ref[...].astype(F32)).astype(BF)
    rows = lax.broadcasted_iota(jnp.int32, (TEXT, TILE), 0)
    live = rows < meta[2]
    keys = [prev[:, :DH], own[:, :DH], nxt[:, :DH], tk_ref[0]]
    vals = [prev[:, DH:], own[:, DH:], nxt[:, DH:], tv_ref[0]]
    scores = [dot(k, q, 1, 1) for k in keys]
    scores[0] = jnp.where(meta[0] > 0, scores[0], -jnp.inf)
    scores[2] = jnp.where(meta[1] > 0, scores[2], -jnp.inf)
    scores[3] = jnp.where(live, scores[3], -jnp.inf)
    top = jnp.max(scores[1], axis=0, keepdims=True)
    for n in (0, 2, 3):
        top = jnp.maximum(top, jnp.max(scores[n], axis=0, keepdims=True))
    powers = [jnp.exp2((s - top) * EXP_SCALE) for s in scores]
    total = sum(jnp.sum(p, axis=0, keepdims=True) for p in powers)
    inverse = 1.0 / total
    probs = [p * inverse for p in powers]
    probs_b = [p.astype(BF) for p in probs]
    dprobs = [dot(v, cot, 1, 1) for v in vals]
    delta = sum(
        jnp.sum(p.astype(F32) * d, axis=0, keepdims=True) for p, d in zip(probs_b, dprobs)
    )
    dscores = [(p * (d - delta) * SCALE).astype(BF) for p, d in zip(probs, dprobs)]
    grad = dot(keys[0], dscores[0], 0, 0)
    for n in (1, 2, 3):
        grad += dot(keys[n], dscores[n], 0, 0)
    swap[:TILE] = grad.T.astype(BF)
    for n, out in ((0, dprev), (1, down), (2, dnext)):
        out[:, :DH] = dot(dscores[n], q, 1, 0).astype(out.dtype)
        out[:, DH:] = dot(probs_b[n], cot, 1, 0).astype(out.dtype)
    text_key = dot(dscores[3], q, 1, 0).astype(BF)
    text_value = dot(probs_b[3], cot, 1, 0).astype(BF)
    first = meta[3] == 0
    keep[...] = jnp.where(first, text_key, text_value)
    swap[TILE:] = jnp.where(first, text_value, text_key)


def attention(sample, meta, adv, q, prev, own, nxt, text_k, text_v, out_grad):
    kv = pl.BlockSpec((TILE, 2 * DH), lambda h: (0, h))
    tile = pl.BlockSpec((TILE, DH), lambda h: (0, h))
    text = pl.BlockSpec((1, TEXT, DH), lambda h: (sample, 0, h))
    return pl.pallas_call(
        attention_kernel,
        grid=(HEADS_DEV,),
        in_specs=[
            SMEM,
            SMEM,
            tile,
            kv,
            kv,
            kv,
            text,
            text,
            pl.BlockSpec((TILE, DH), lambda h: (sample, h)),
        ],
        out_specs=[
            pl.BlockSpec((TILE + TEXT, DH), lambda h: (0, h)),
            kv,
            kv,
            kv,
            pl.BlockSpec((TEXT, DH), lambda h: (0, h)),
        ],
        out_shape=[
            jax.ShapeDtypeStruct((TILE + TEXT, CH), BF),
            jax.ShapeDtypeStruct((TILE, 2 * CH), BF),
            jax.ShapeDtypeStruct((TILE, 2 * CH), F32),
            jax.ShapeDtypeStruct((TILE, 2 * CH), BF),
            jax.ShapeDtypeStruct((TEXT, CH), BF),
        ],
        compiler_params=pltpu.CompilerParams(vmem_limit_bytes=24 * MIB),
        cost_estimate=pl.CostEstimate(
            flops=20 * 3 * 384 * 1408 * 128, bytes_accessed=8 * MIB, transcendentals=3 * 384 * 1408
        ),
        name="attention",
    )(meta, adv, q, prev, own, nxt, text_k, text_v, out_grad)


def hidden_kernel(meta, swap, down, low, high, w, grads, *outs):
    a, y = (meta[0], meta[1])
    kv = down[...] + low[...].astype(F32) + high[...].astype(F32)
    for h in range(HEADS_DEV):
        grads[:, h * DH : (h + 1) * DH] = kv[:, 2 * h * DH : (2 * h + 1) * DH].astype(BF)
        grads[:, CH + h * DH : CH + (h + 1) * DH] = kv[
            :, (2 * h + 1) * DH : (2 * h + 2) * DH
        ].astype(BF)
    g = [swap[:TILE], grads[:, :CH], grads[:, CH:]]
    for d in (2, 1, 3, 0):
        yj = (y + d) & 3
        j0, j1 = (a * 4 + yj, (1 - a) * 4 + yj)
        part = None
        for c in range(3):
            wc = jnp.concatenate([w[c, j0], w[c, j1]], axis=0)
            term = dot(g[c], wc, 1, 1)
            part = term if part is None else part + term
        if d == 2:
            outs[0][...] = part[:, :CH].astype(BF)
            outs[1][...] = part[:, CH:].astype(BF)
        else:
            out = outs[{1: 2, 3: 3, 0: 4}[d]]
            out[0] = part[:, :CH].astype(BF)
            out[1] = part[:, CH:].astype(BF)


def hidden_parts(meta, swap, down, low, high, w):
    one = jax.ShapeDtypeStruct((TILE, CH), BF)
    two = jax.ShapeDtypeStruct((2, TILE, CH), BF)
    return pl.pallas_call(
        hidden_kernel,
        in_specs=[SMEM] + [VMEM] * 5,
        out_specs=[VMEM] * 6,
        out_shape=[jax.ShapeDtypeStruct((TILE, 2 * CH), BF), one, one, two, two, two],
        compiler_params=pltpu.CompilerParams(vmem_limit_bytes=16 * MIB),
        cost_estimate=pl.CostEstimate(
            flops=2 * TILE * 3072 * 1152, bytes_accessed=14 * MIB, transcendentals=0
        ),
        name="hidden_parts",
    )(meta, swap, down, low, high, w)


def add(*terms):
    total = terms[0].astype(F32)
    for term in terms[1:]:
        total = total + term.astype(F32)
    return total.astype(BF)


def hidden_reduce(far_same, far_flip, up, down, here):
    got_same = head_move(far_same, 0, 3)
    got_flip = head_move(far_flip, 0, 1)
    up = jnp.stack([up[0], add(up[1], got_flip)])
    down = jnp.stack([add(down[0], got_same), down[1]])
    got_up = head_move(up, 0, 1)
    got_down = head_move(down, 0, 3)
    across = head_move(add(here[1], got_up[1], got_down[1]), 1, 0)
    return add(here[0], got_up[0], got_down[0], across)


def query_weight_kernel(meta, x0, x1, p0, p1, g0, g1, h0, h1, keep0, keep1, *rest):
    outs, text = (rest[:4], rest[4])
    z = meta[3]
    g = jnp.concatenate([r[:TILE] for r in (g0, g1, h0, h1)], axis=0)
    for s, (keep, got) in enumerate(((keep0, h0), (keep1, h1))):
        both = (keep[...].astype(F32) + got[TILE:].astype(F32)).astype(BF)
        text[2 * s] = both[: TEXT // 2]
        text[2 * s + 1] = both[TEXT // 2 :]
    for d in (2, 1, 3, 0):
        j = (z + d) & 3
        x = jnp.concatenate([x0[j], x1[j], p0[j], p1[j]], axis=0)
        outs[d][:CH] = dot(x, g, 0, 0).astype(BF)
        outs[d][CH:] = text[j]


def query_weight_parts(meta, *arrays):
    shape = jax.ShapeDtypeStruct((CH + TEXT // 2, CH), BF)
    return pl.pallas_call(
        query_weight_kernel,
        in_specs=[SMEM] + [VMEM] * 10,
        out_specs=[VMEM] * 4,
        out_shape=[shape] * 4,
        scratch_shapes=[pltpu.VMEM((4, TEXT // 2, CH), BF)],
        compiler_params=pltpu.CompilerParams(vmem_limit_bytes=16 * MIB),
        cost_estimate=pl.CostEstimate(
            flops=2 * 768 * 3072 * 384, bytes_accessed=10 * MIB, transcendentals=0
        ),
        name="query_weight_parts",
    )(meta, *arrays)


def weight_kernel(meta, x0, x1, p0, p1, g0, g1, h0, h1, *outs):
    z = meta[3]
    g = jnp.concatenate([g0[...], g1[...], h0[...], h1[...]], axis=0)
    for d in (2, 1, 3, 0):
        j = (z + d) & 3
        x = jnp.concatenate([x0[j], x1[j], p0[j], p1[j]], axis=0)
        outs[d][...] = dot(x, g, 0, 0).astype(BF)


def weight_parts(meta, *arrays):
    shape = jax.ShapeDtypeStruct((CH, 2 * CH), BF)
    return pl.pallas_call(
        weight_kernel,
        in_specs=[SMEM] + [VMEM] * 8,
        out_specs=[VMEM] * 4,
        out_shape=[shape] * 4,
        compiler_params=pltpu.CompilerParams(vmem_limit_bytes=20 * MIB),
        cost_estimate=pl.CostEstimate(
            flops=2 * 768 * 3072 * 768, bytes_accessed=13 * MIB, transcendentals=0
        ),
        name="weight_parts",
    )(meta, *arrays)


def z_sum(parts):
    got = [slab_move(parts[d], d, 0, 0) for d in (2, 1, 3)]
    return add(parts[0], *got)


def weight_home(total, x_lo, core):
    halves = total.reshape(2, CH // 2, 3 * CH)
    home = x_lo == core
    near = lax.dynamic_index_in_dim(halves, jnp.where(home, 1 - core, core), 0, keepdims=False)
    far = lax.dynamic_index_in_dim(halves, jnp.where(home, core, 1 - core), 0, keepdims=False)
    first, second = ([], [])
    for s in range(16):
        z, x, c = (s // 4, s // 2 % 2, s % 2)
        if x == c:
            first.append((s, z * 4 + x * 2 + 1 - c))
        else:
            first.append((s, z * 4 + (1 - x) * 2 + c))
            second.append((s, z * 4 + (1 - x) * 2 + 1 - c))
    got_first = lax.ppermute(near, "slab", first)
    got_second = lax.ppermute(far, "slab", second)
    return add(jnp.where(home, far, got_second), got_first)


def text_spread(quarter, core):
    z = lax.axis_index("slab") // 4
    quarter = add(quarter, slab_move(quarter, 0, 1, 0))
    full = jnp.zeros((4, TEXT // 2, CH), BF)
    full = lax.dynamic_update_index_in_dim(full, quarter, z, 0)
    for d in (2, 1, 3):
        full = lax.dynamic_update_index_in_dim(full, slab_move(quarter, d, 0, 0), (z - d) % 4, 0)
    full = full.reshape(SAMPLES, TEXT, CH)
    twin = slab_move(full, 0, 0, 1)
    key = jnp.where(core == 0, full, twin)
    value = jnp.where(core == 0, twin, full)
    return jnp.stack([key, value], axis=2)


def gather_chunks(own, after):
    flip = head_move(own, 1, 0)
    if after is not None:
        own, _ = lax.optimization_barrier((own, after))
    below = head_move(own, 0, 1)
    above = head_move(own, 0, 3)
    flip_below = head_move(flip, 0, 1)
    flip_above = head_move(flip, 0, 3)
    far = head_move(below, 0, 1)
    far_flip = head_move(flip_above, 0, 3)
    return [own, flip, below, above, flip_below, flip_above, far, far_flip]


def body(hidden, w_qkv, text_keys, text_values, text_len, advantage, out_grad, tile_lists):
    slab = lax.axis_index("slab")
    head = lax.axis_index("head")
    core = slab % 2
    x_lo = slab // 2 % 2
    place = jnp.stack([head // 4, head % 4, core, slab // 4]).astype(jnp.int32)
    w = jnp.transpose(w_qkv, (1, 0, 2)).reshape(3, 8, CH, CH)
    index = jnp.arange(SAMPLES, dtype=jnp.int32)[:, None] + slab * SAMPLES
    has_prev = jnp.any((tile_lists == index - SAMPLES) & (tile_lists >= 0), axis=1)
    has_next = jnp.any(tile_lists == index + SAMPLES, axis=1)
    flags = jnp.stack(
        [
            has_prev.astype(jnp.int32),
            has_next.astype(jnp.int32),
            text_len,
            jnp.broadcast_to(core, (SAMPLES,)),
        ],
        axis=1,
    )
    swaps, keeps, grads, mines, theirs, hidden_grads = ([], [], [], [], [], [])
    after = None
    for s in range(SAMPLES):
        chunks = gather_chunks(hidden[s * TILE : (s + 1) * TILE], after)
        after = chunks[4]
        q, kv, mine, other = project(place, chunks, w)
        mines.append(mine)
        prev = slab_step(kv, 1)
        nxt = slab_step(kv, -1)
        q, their = lax.optimization_barrier((q, slab_move(other, 0, 0, 1)))
        theirs.append(their)
        swap, dprev, down, dnext, keep = attention(
            s, flags[s], advantage[s : s + 1], q, prev, kv, nxt, text_keys, text_values, out_grad
        )
        swaps.append(swap)
        keeps.append(keep)
        low = slab_step(dnext, 1)
        high = slab_step(dprev, -1)
        made = hidden_parts(place, swap, down, low, high, w)
        grads.append(made[0])
        hidden_grads.append(hidden_reduce(*made[1:]))
    got = [slab_move(g, 0, 0, 1) for g in swaps]
    twins = [slab_move(g, 0, 0, 1) for g in grads]
    query_total = z_sum(query_weight_parts(place, *mines, *theirs, *swaps, *got, *keeps))
    text_grad = text_spread(query_total[CH:], core)
    total = z_sum(weight_parts(place, *mines, *theirs, *grads, *twins))
    total = jnp.concatenate([query_total[:CH], total], axis=1)
    weight_grad = weight_home(total, x_lo, core).reshape(CH // 2, 3, CH)
    hidden_grad = jnp.concatenate(hidden_grads, axis=0)
    return (hidden_grad, weight_grad, text_grad)


def solution(mesh):
    in_specs = (
        P("slab", "head"),
        P(None, None, "head"),
        P(None, None, "head"),
        P(None, None, "head"),
        P(),
        P(),
        P("slab", "head"),
        P("slab", None),
    )
    out_specs = (P("slab", "head"), P("slab", None, "head"), P(None, None, None, "head"))
    return jax.shard_map(body, mesh=mesh, in_specs=in_specs, out_specs=out_specs, check_vma=False)
```

```python
import functools
import math

import jax
import jax.numpy as jnp
from jax import lax
from jax.experimental import pallas as pl
from jax.experimental.pallas import tpu as pltpu
from jax.sharding import PartitionSpec as P

DH = 128
TILE = 384
SAMPLES = 2
HEADS_DEV = 3
CH = 384
TEXT = 256
BF = jnp.bfloat16
F32 = jnp.float32
SCALE = 1.0 / math.sqrt(DH)
EXP_SCALE = SCALE * math.log2(math.e)
MIB = 1024 * 1024
COST = pl.CostEstimate(flops=10**6, bytes_accessed=10**4, transcendentals=0)

VMEM = pl.BlockSpec(memory_space=pltpu.VMEM)
SMEM = pl.BlockSpec(memory_space=pltpu.SMEM)


def dot(a, b, ca, cb):
    return lax.dot_general(a, b, (((ca,), (cb,)), ((), ())), preferred_element_type=F32)


def head_move(x, dx, dy):
    pairs = [(h, ((h // 4) ^ dx) * 4 + (h + dy) % 4) for h in range(8)]
    return lax.ppermute(x, "head", pairs)


def slab_move(x, dz, dx, dc):
    pairs = [
        (s, ((s // 4 + dz) % 4) * 4 + ((s // 2 % 2) ^ dx) * 2 + ((s % 2) ^ dc)) for s in range(16)
    ]
    return lax.ppermute(x, "slab", pairs)


def slab_step(x, distance):
    pairs = [(i, (i + distance) % 16) for i in range(16)]
    return lax.ppermute(x, "slab", pairs)


def place():
    slab, head = (lax.axis_index("slab"), lax.axis_index("head"))
    return (head >> 2, head & 3, slab >> 2, (slab >> 1) & 1, slab & 1)


def call(kernel, name, arrays, shapes, limit, scratch=(), **options):
    return pl.pallas_call(
        kernel,
        in_specs=[VMEM] * len(arrays),
        out_specs=[VMEM] * len(shapes),
        out_shape=[jax.ShapeDtypeStruct(shape, BF) for shape in shapes],
        scratch_shapes=list(scratch),
        compiler_params=pltpu.CompilerParams(vmem_limit_bytes=limit * MIB),
        cost_estimate=COST,
        name=name,
        **options,
    )(*arrays)


def total(*refs):
    value = refs[0].astype(F32)
    for ref in refs[1:]:
        value = value + ref.astype(F32)
    return value.astype(BF)


PAIRS = ((0, 0, 1), (3, 2, 4), (1, 3, 5), (2, 6, 7))


def project_kernel(*refs):
    chunks, (w, q_out, kv_out, mine, other, acc) = (refs[:8], refs[8:])
    a, y, _, _, core = place()
    for n, (d, r0, r1) in enumerate(PAIRS):
        yj = (y + d) & 3
        pair = ((a, chunks[r0]), (1 - a, chunks[r1]))
        own = ((yj ^ core) & 1) == 0
        for r, ref in pair:
            z = (r * 4 + yj) >> 1

            @pl.when(own)
            def _():
                mine[z] = ref[...]

            @pl.when(jnp.logical_not(own))
            def _():
                other[z] = ref[...]

        x = jnp.concatenate([ref[...] for _, ref in pair], axis=1)
        for c in range(3):
            wc = jnp.concatenate([w[c, r, yj] for r, _ in pair], axis=0)
            part = dot(x, wc, 1, 0)
            if n == 0:
                acc[c] = part
            else:
                acc[c] += part

    q_out[...] = acc[0].astype(BF)
    for h in range(HEADS_DEV):
        cols = slice(h * DH, (h + 1) * DH)
        kv_out[:, 2 * h * DH : (2 * h + 1) * DH] = acc[1, :, cols].astype(BF)
        kv_out[:, (2 * h + 1) * DH : (2 * h + 2) * DH] = acc[2, :, cols].astype(BF)


def project(chunks, w):
    return call(
        project_kernel,
        "project",
        [*chunks, w],
        [(TILE, CH), (TILE, 2 * CH), (4, TILE, CH), (4, TILE, CH)],
        4,
        [pltpu.VMEM((3, TILE, CH), F32)],
    )


def attention_kernel(
    sample,
    lists,
    lengths,
    adv,
    q_ref,
    prev,
    own,
    nxt,
    tk_ref,
    tv_ref,
    og_ref,
    swap,
    dprev,
    down,
    dnext,
    keep,
):
    slab = lax.axis_index("slab")
    tile = slab * SAMPLES + sample
    before, after = (False, False)
    for n in range(lists.shape[1]):
        before = before | (lists[sample, n] == tile - SAMPLES)
        after = after | (lists[sample, n] == tile + SAMPLES)
    before = before & (slab > 0)
    q = q_ref[...]
    cot = (adv[sample] * og_ref[...].astype(F32)).astype(BF)
    rows = lax.broadcasted_iota(jnp.int32, (TEXT, TILE), 0)
    live = rows < lengths[sample]
    keys = [prev[:, :DH], own[:, :DH], nxt[:, :DH], tk_ref[0]]
    vals = [prev[:, DH:], own[:, DH:], nxt[:, DH:], tv_ref[0]]
    scores = [dot(k, q, 1, 1) for k in keys]
    scores[0] = jnp.where(before, scores[0], -jnp.inf)
    scores[2] = jnp.where(after, scores[2], -jnp.inf)
    scores[3] = jnp.where(live, scores[3], -jnp.inf)
    top = jnp.max(scores[1], axis=0, keepdims=True)
    for n in (0, 2, 3):
        top = jnp.maximum(top, jnp.max(scores[n], axis=0, keepdims=True))
    powers = [jnp.exp2((s - top) * EXP_SCALE) for s in scores]
    total = sum(jnp.sum(p, axis=0, keepdims=True) for p in powers)
    inverse = 1.0 / total
    probs = [p * inverse for p in powers]
    probs_b = [p.astype(BF) for p in probs]
    dprobs = [dot(v, cot, 1, 1) for v in vals]
    delta = sum(
        jnp.sum(p.astype(F32) * d, axis=0, keepdims=True) for p, d in zip(probs_b, dprobs)
    )
    dscores = [(p * (d - delta) * SCALE).astype(BF) for p, d in zip(probs, dprobs)]
    grad = dot(keys[0], dscores[0], 0, 0)
    for n in (1, 2, 3):
        grad += dot(keys[n], dscores[n], 0, 0)
    swap[:TILE] = grad.T.astype(BF)
    for n, out in ((0, dprev), (1, down), (2, dnext)):
        out[:, :DH] = dot(dscores[n], q, 1, 0).astype(out.dtype)
        out[:, DH:] = dot(probs_b[n], cot, 1, 0).astype(out.dtype)
    text_key = dot(dscores[3], q, 1, 0).astype(BF)
    text_value = dot(probs_b[3], cot, 1, 0).astype(BF)
    first = (slab & 1) == 0
    keep[...] = jnp.where(first, text_key, text_value)
    swap[TILE:] = jnp.where(first, text_value, text_key)


def attention(sample, scalars, q, prev, own, nxt, text_k, text_v, out_grad):
    kv = pl.BlockSpec((TILE, 2 * DH), lambda h: (0, h))
    tile = pl.BlockSpec((TILE, DH), lambda h: (0, h))
    text = pl.BlockSpec((1, TEXT, DH), lambda h: (sample, 0, h))
    return pl.pallas_call(
        functools.partial(attention_kernel, sample),
        grid=(HEADS_DEV,),
        in_specs=[
            SMEM,
            SMEM,
            SMEM,
            tile,
            kv,
            kv,
            kv,
            text,
            text,
            pl.BlockSpec((TILE, DH), lambda h: (sample, h)),
        ],
        out_specs=[
            pl.BlockSpec((TILE + TEXT, DH), lambda h: (0, h)),
            kv,
            kv,
            kv,
            pl.BlockSpec((TEXT, DH), lambda h: (0, h)),
        ],
        out_shape=[
            jax.ShapeDtypeStruct((TILE + TEXT, CH), BF),
            jax.ShapeDtypeStruct((TILE, 2 * CH), BF),
            jax.ShapeDtypeStruct((TILE, 2 * CH), F32),
            jax.ShapeDtypeStruct((TILE, 2 * CH), BF),
            jax.ShapeDtypeStruct((TEXT, CH), BF),
        ],
        compiler_params=pltpu.CompilerParams(vmem_limit_bytes=12 * MIB),
        cost_estimate=COST,
        name="attention",
    )(*scalars, q, prev, own, nxt, text_k, text_v, out_grad)


REDUCE_ORDER = (2, 1, 3, 0)


def hidden_kernel(swap, kv, w, *outs):
    a, y, _, _, _ = place()
    keys = [kv[:, 2 * h * DH : (2 * h + 1) * DH] for h in range(HEADS_DEV)]
    vals = [kv[:, (2 * h + 1) * DH : (2 * h + 2) * DH] for h in range(HEADS_DEV)]
    g = [swap[:TILE], jnp.concatenate(keys, axis=1), jnp.concatenate(vals, axis=1)]
    for n, d in enumerate(REDUCE_ORDER):
        yj = (y + d) & 3
        part = None
        for c in range(3):
            wc = jnp.concatenate([w[c, a, yj], w[c, 1 - a, yj]], axis=0)
            term = dot(g[c], wc, 1, 1)
            part = term if part is None else part + term
        if d == 2:
            outs[0][...] = part[:, :CH].astype(BF)
            outs[1][...] = part[:, CH:].astype(BF)
        else:
            outs[n + 1][0] = part[:, :CH].astype(BF)
            outs[n + 1][1] = part[:, CH:].astype(BF)


def hidden_parts(swap, kv, w):
    one, two = ((TILE, CH), (2, TILE, CH))
    return call(hidden_kernel, "hidden_parts", [swap, kv, w], [one, one, two, two, two], 4)


def bundle_kernel(got_same, got_flip, up, down, up_out, down_out):
    up_out[0] = up[0]
    up_out[1] = total(up[1], got_flip[...])
    down_out[0] = total(down[0], got_same[...])
    down_out[1] = down[1]


def hidden_far(far_same, far_flip, up, down, here):
    return (head_move(far_same, 0, 3), head_move(far_flip, 0, 1), up, down, here)


def hidden_sides(got_same, got_flip, up, down, here):
    two = (2, TILE, CH)
    up, down = call(
        bundle_kernel,
        "hidden_bundle",
        [got_same, got_flip, up, down],
        [two, two],
        4,
        input_output_aliases={2: 0, 3: 1},
    )
    return (here, head_move(up, 0, 1), head_move(down, 0, 3))


def across_kernel(here, up, down, out):
    out[...] = total(here[1], up[1], down[1])


def hidden_across(terms):
    return head_move(call(across_kernel, "hidden_across", terms, [(TILE, CH)], 4)[0], 1, 0)


def hidden_final_kernel(*refs):
    out = refs[-1]
    for s in range(SAMPLES):
        here, up, down, across = refs[4 * s : 4 * s + 4]
        out[s * TILE : (s + 1) * TILE] = total(here[0], up[0], down[0], across[...])


def query_weight_kernel(x0, x1, p0, p1, g0, g1, h0, h1, keep0, keep1, *rest):
    outs, text = (rest[:4], rest[4])
    _, _, z, _, _ = place()
    g = jnp.concatenate([r[:TILE] for r in (g0, g1, h0, h1)], axis=0)
    for s, (keep, got) in enumerate(((keep0, h0), (keep1, h1))):
        both = total(keep[...], got[TILE:])
        text[2 * s] = both[: TEXT // 2]
        text[2 * s + 1] = both[TEXT // 2 :]
    for d in (2, 1, 3, 0):
        j = (z + d) & 3
        x = jnp.concatenate([x0[j], x1[j], p0[j], p1[j]], axis=0)
        outs[d][:CH] = dot(x, g, 0, 0).astype(BF)
        outs[d][CH:] = text[j]


def query_weight_parts(*arrays):
    return call(
        query_weight_kernel,
        "query_weight_parts",
        arrays,
        [(CH + TEXT // 2, CH)] * 4,
        4,
        [pltpu.VMEM((4, TEXT // 2, CH), BF)],
    )


def weight_kernel(x0, x1, p0, p1, g0, g1, h0, h1, *outs):
    _, _, z, _, _ = place()
    g = jnp.concatenate([g0[...], g1[...], h0[...], h1[...]], axis=0)
    for d in (2, 1, 3, 0):
        j = (z + d) & 3
        x = jnp.concatenate([x0[j], x1[j], p0[j], p1[j]], axis=0)
        part = dot(x, g, 0, 0).astype(BF)
        for h in range(HEADS_DEV):
            key, value = (2 * h * DH, (2 * h + 1) * DH)
            outs[d][:, h * DH : (h + 1) * DH] = part[:, key : key + DH]
            outs[d][:, CH + h * DH : CH + (h + 1) * DH] = part[:, value : value + DH]


def weight_parts(*arrays):
    return call(weight_kernel, "weight_parts", arrays, [(CH, 2 * CH)] * 4, 6)


def z_moves(parts):
    return [slab_move(parts[d], d, 0, 0) for d in (2, 1, 3)]


def weight_halves_kernel(*refs):
    query, rest, (near, far) = (refs[:4], refs[4:8], refs[8:])
    _, _, _, x, core = place()
    home = x == core
    for half in range(2):
        rows = slice(half * CH // 2, (half + 1) * CH // 2)
        q = total(*[r[rows] for r in query])
        kv = total(*[r[rows] for r in rest])
        is_far = (core == half) == home

        @pl.when(is_far)
        def _():
            far[:, :CH] = q
            far[:, CH:] = kv

        @pl.when(jnp.logical_not(is_far))
        def _():
            near[:, :CH] = q
            near[:, CH:] = kv


def weight_final_kernel(far, got_first, got_second, out):
    _, _, _, x, core = place()
    for c in range(3):
        cols = slice(c * CH, (c + 1) * CH)
        kept = jnp.where(x == core, far[:, cols], got_second[:, cols])
        out[c] = total(kept, got_first[:, cols])


def weight_home(query, rest):
    half = (CH // 2, 3 * CH)
    near, far = call(weight_halves_kernel, "weight_halves", [*query, *rest], [half, half], 6)
    first, second = ([], [])
    for s in range(16):
        z, x, c = (s // 4, s // 2 % 2, s % 2)
        if x == c:
            first.append((s, z * 4 + x * 2 + 1 - c))
        else:
            first.append((s, z * 4 + (1 - x) * 2 + c))
            second.append((s, z * 4 + (1 - x) * 2 + 1 - c))
    got_first = lax.ppermute(near, "slab", first)
    got_second = lax.ppermute(far, "slab", second)
    out = call(
        weight_final_kernel, "weight_final", [far, got_first, got_second], [(3, CH // 2, CH)], 4
    )[0]
    return jnp.transpose(out, (1, 0, 2))


def text_sum_kernel(*refs):
    refs[-1][...] = total(*[r[CH:] for r in refs[:-1]])


def text_pair_kernel(one, two, out):
    out[...] = total(one[...], two[...])


def text_full_kernel(own, far, below, above, out):
    _, _, z, _, _ = place()
    for d, ref in ((0, own), (2, far), (1, below), (3, above)):
        out[(z - d) & 3] = ref[...]


def text_final_kernel(full, twin, key, value):
    _, _, _, _, core = place()
    key[...] = jnp.where(core == 0, full[...], twin[...])
    value[...] = jnp.where(core == 0, twin[...], full[...])


def text_spread(parts):
    shape = (TEXT // 2, CH)
    quarter = call(text_sum_kernel, "text_sum", parts, [shape], 4)[0]
    pair = [quarter, slab_move(quarter, 0, 1, 0)]
    quarter = call(text_pair_kernel, "text_pair", pair, [shape], 4)[0]
    full = call(text_full_kernel, "text_full", [quarter, *z_moves([quarter] * 4)], [(4, *shape)], 4)[0]
    both = [full, slab_move(full, 0, 0, 1)]
    pair = call(text_final_kernel, "text_final", both, [(4, *shape)] * 2, 4)
    return jnp.stack([part.reshape(SAMPLES, TEXT, CH) for part in pair], axis=2)


def gather_chunks(own, after):
    flip = head_move(own, 1, 0)
    below = head_move(own, 0, 1)
    above = head_move(own, 0, 3)
    flip_below = head_move(flip, 0, 1)
    flip_above = head_move(flip, 0, 3)
    if after is not None:
        below, flip_above, _ = lax.optimization_barrier((below, flip_above, after))
    far = head_move(below, 0, 1)
    far_flip = head_move(flip_above, 0, 3)
    return [own, flip, below, above, flip_below, flip_above, far, far_flip]


def body(hidden, w_qkv, text_keys, text_values, text_len, advantage, out_grad, tile_lists):
    w = jnp.transpose(w_qkv, (1, 0, 2)).reshape(3, 2, 4, CH, CH)
    scalars = (tile_lists, text_len, advantage)
    swaps, keeps, grads, mines, theirs = ([], [], [], [], [])
    after = None
    for s in range(SAMPLES):
        chunks = gather_chunks(hidden[s * TILE : (s + 1) * TILE], after)
        after = chunks[5]
        q, kv, mine, other = project(chunks, w)
        mines.append(mine)
        prev = slab_step(kv, 1)
        nxt = slab_step(kv, -1)
        other, prev, nxt = lax.optimization_barrier((other, prev, nxt))
        their = slab_move(other, 0, 0, 1)
        swap, dprev, down, dnext, keep = attention(
            s, scalars, q, prev, kv, nxt, text_keys, text_values, out_grad
        )
        dprev, dnext, their = lax.optimization_barrier((dprev, dnext, their))
        theirs.append(their)
        swaps.append(swap)
        keeps.append(keep)
        low = slab_step(dnext, 1)
        high = slab_step(dprev, -1)
        grads.append(total(down, low, high))
    got = [slab_move(g, 0, 0, 1) for g in swaps]
    twins = [slab_move(g, 0, 0, 1) for g in grads]
    query = query_weight_parts(*mines, *theirs, *swaps, *got, *keeps)
    query = [query[0], *z_moves(query)]
    first = hidden_sides(*hidden_far(*hidden_parts(swaps[0], grads[0], w)))
    rest = weight_parts(*mines, *theirs, *grads, *twins)
    grad, rest = lax.optimization_barrier((grads[1], rest))
    rest = [rest[0], *z_moves(rest)]
    second = hidden_far(*hidden_parts(swaps[1], grad, w))
    text_parts, second, rest[2] = lax.optimization_barrier((query, second, rest[2]))
    second = hidden_sides(*second)
    ends = [*first, hidden_across(first), *second, hidden_across(second)]
    hidden_grad = call(hidden_final_kernel, "hidden_final", ends, [(SAMPLES * TILE, CH)], 4)[0]
    text_grad = text_spread(text_parts)
    weight_grad = weight_home(query, rest)
    return (hidden_grad, weight_grad, text_grad)


def solution(mesh):
    in_specs = (
        P("slab", "head"),
        P(None, None, "head"),
        P(None, None, "head"),
        P(None, None, "head"),
        P(),
        P(),
        P("slab", "head"),
        P("slab", None),
    )
    out_specs = (P("slab", "head"), P("slab", None, "head"), P(None, None, None, "head"))
    return jax.shard_map(body, mesh=mesh, in_specs=in_specs, out_specs=out_specs, check_vma=False)
```

```python
import functools
import math

import jax
import jax.numpy as jnp
from jax import lax
from jax.experimental import pallas as pl
from jax.experimental.pallas import tpu as pltpu
from jax.sharding import PartitionSpec as P

DH = 128
TILE = 384
SAMPLES = 2
HEADS_DEV = 3
CH = 384
TEXT = 256
BF = jnp.bfloat16
F32 = jnp.float32
SCALE = 1.0 / math.sqrt(DH)
EXP_SCALE = SCALE * math.log2(math.e)
MIB = 1024 * 1024
COST = pl.CostEstimate(flops=10**6, bytes_accessed=10**4, transcendentals=0)

VMEM = pl.BlockSpec(memory_space=pltpu.VMEM)
SMEM = pl.BlockSpec(memory_space=pltpu.SMEM)


def dot(a, b, ca, cb):
    return lax.dot_general(a, b, (((ca,), (cb,)), ((), ())), preferred_element_type=F32)


def head_move(x, dx, dy):
    pairs = [(h, ((h // 4) ^ dx) * 4 + (h + dy) % 4) for h in range(8)]
    return lax.ppermute(x, "head", pairs)


def slab_move(x, dz, dx, dc):
    pairs = [
        (s, ((s // 4 + dz) % 4) * 4 + ((s // 2 % 2) ^ dx) * 2 + ((s % 2) ^ dc)) for s in range(16)
    ]
    return lax.ppermute(x, "slab", pairs)


def slab_step(x, distance):
    pairs = [(i, (i + distance) % 16) for i in range(16)]
    return lax.ppermute(x, "slab", pairs)


def place():
    slab, head = (lax.axis_index("slab"), lax.axis_index("head"))
    return (head >> 2, head & 3, slab >> 2, (slab >> 1) & 1, slab & 1)


def call(kernel, name, arrays, shapes, limit, scratch=(), **options):
    return pl.pallas_call(
        kernel,
        in_specs=[VMEM] * len(arrays),
        out_specs=[VMEM] * len(shapes),
        out_shape=[jax.ShapeDtypeStruct(shape, BF) for shape in shapes],
        scratch_shapes=list(scratch),
        compiler_params=pltpu.CompilerParams(vmem_limit_bytes=limit * MIB),
        cost_estimate=COST,
        name=name,
        **options,
    )(*arrays)


def total(*refs):
    value = refs[0].astype(F32)
    for ref in refs[1:]:
        value = value + ref.astype(F32)
    return value.astype(BF)


ROWS = SAMPLES * TILE
EARLY = ((0, 0, 1), (3, 2, 4), (1, 3, 5), (2, 6, None))


def place_chunk(ref, a, yj, core, mine, other):
    z = (a * 4 + yj) >> 1
    own = ((yj ^ core) & 1) == 0

    @pl.when(own)
    def _():
        mine[z] = ref[...]

    @pl.when(jnp.logical_not(own))
    def _():
        other[z] = ref[...]


def project_early_kernel(*refs):
    chunks, (w, acc, mine, other) = (refs[:7], refs[7:])
    a, y, _, _, core = place()
    for n, (d, r0, r1) in enumerate(EARLY):
        yj = (y + d) & 3
        pair = [(a, chunks[r0])] + ([] if r1 is None else [(1 - a, chunks[r1])])
        for r, ref in pair:
            place_chunk(ref, r, yj, core, mine, other)
        x = jnp.concatenate([ref[...] for _, ref in pair], axis=1)
        for c in range(3):
            wc = jnp.concatenate([w[c, r, yj] for r, _ in pair], axis=0)
            part = dot(x, wc, 1, 0)
            if n == 0:
                acc[c] = part
            else:
                acc[c] += part


def project_late_kernel(first, second, w, acc, mine_in, other_in, q_out, *refs):
    kv_outs, (mine, other, last) = (refs[:SAMPLES], refs[SAMPLES:])
    a, y, _, _, core = place()
    yj = (y + 2) & 3
    last[:TILE] = first[...]
    last[TILE:] = second[...]
    place_chunk(last, 1 - a, yj, core, mine, other)
    for c in (1, 2, 0):
        part = (acc[c] + dot(last[...], w[c, 1 - a, yj], 1, 0)).astype(BF)
        if c == 0:
            q_out[...] = part
            continue
        for s, kv_out in enumerate(kv_outs):
            for h in range(HEADS_DEV):
                at = (2 * h + c - 1) * DH
                kv_out[:, at : at + DH] = part[s * TILE : (s + 1) * TILE, h * DH : (h + 1) * DH]


def project(hidden, w):
    flip = head_move(hidden, 1, 0)
    below = head_move(hidden, 0, 1)
    above = head_move(hidden, 0, 3)
    flip, below, above = lax.optimization_barrier((flip, below, above))
    flip_below = head_move(below, 1, 0)
    flip_above = head_move(flip, 0, 3)
    far = head_move(below, 0, 1)
    flip_below, flip_above, far = lax.optimization_barrier((flip_below, flip_above, far))
    last = [head_move(flip_below[:TILE], 0, 1), head_move(flip_above[TILE:], 0, 3)]
    chunks = [hidden, flip, below, above, flip_below, flip_above, far]
    held = [jax.ShapeDtypeStruct((4, ROWS, CH), BF)] * 2
    acc, mine, other = pl.pallas_call(
        project_early_kernel,
        in_specs=[VMEM] * 8,
        out_specs=[VMEM] * 3,
        out_shape=[jax.ShapeDtypeStruct((3, ROWS, CH), F32), *held],
        compiler_params=pltpu.CompilerParams(vmem_limit_bytes=6 * MIB),
        cost_estimate=COST,
        name="project_early",
    )(*chunks, w)
    shapes = [(ROWS, CH), (TILE, 2 * CH), (TILE, 2 * CH), (4, ROWS, CH), (4, ROWS, CH)]
    return call(
        project_late_kernel,
        "project_late",
        [*last, w, acc, mine, other],
        shapes,
        6,
        [pltpu.VMEM((ROWS, CH), BF)],
        input_output_aliases={4: 3, 5: 4},
    )


def attention_kernel(
    sample,
    lists,
    lengths,
    adv,
    q_ref,
    prev,
    own,
    nxt,
    tk_ref,
    tv_ref,
    og_ref,
    *refs,
):
    swap, dprev, down, dnext, keep = refs[-5:]
    slab = lax.axis_index("slab")
    tile = slab * SAMPLES + sample
    before, after = (False, False)
    for n in range(lists.shape[1]):
        before = before | (lists[sample, n] == tile - SAMPLES)
        after = after | (lists[sample, n] == tile + SAMPLES)
    before = before & (slab > 0)
    q = q_ref[...]
    cot = (adv[sample] * og_ref[...].astype(F32)).astype(BF)
    rows = lax.broadcasted_iota(jnp.int32, (TEXT, TILE), 0)
    live = rows < lengths[sample]
    keys = [prev[:, :DH], own[:, :DH], nxt[:, :DH], tk_ref[0]]
    vals = [prev[:, DH:], own[:, DH:], nxt[:, DH:], tv_ref[0]]
    scores = [dot(k, q, 1, 1) for k in keys]
    scores[0] = jnp.where(before, scores[0], -jnp.inf)
    scores[2] = jnp.where(after, scores[2], -jnp.inf)
    scores[3] = jnp.where(live, scores[3], -jnp.inf)
    top = jnp.max(scores[1], axis=0, keepdims=True)
    for n in (0, 2, 3):
        top = jnp.maximum(top, jnp.max(scores[n], axis=0, keepdims=True))
    powers = [jnp.exp2((s - top) * EXP_SCALE) for s in scores]
    total = sum(jnp.sum(p, axis=0, keepdims=True) for p in powers)
    inverse = 1.0 / total
    probs = [p * inverse for p in powers]
    probs_b = [p.astype(BF) for p in probs]
    dprobs = [dot(v, cot, 1, 1) for v in vals]
    delta = sum(
        jnp.sum(p.astype(F32) * d, axis=0, keepdims=True) for p, d in zip(probs_b, dprobs)
    )
    dscores = [(p * (d - delta) * SCALE).astype(BF) for p, d in zip(probs, dprobs)]
    grad = dot(keys[0], dscores[0], 0, 0)
    for n in (1, 2, 3):
        grad += dot(keys[n], dscores[n], 0, 0)
    swap[0, :TILE] = grad.T.astype(BF)
    for n, out in ((0, dprev), (1, down), (2, dnext)):
        out[:, :DH] = dot(dscores[n], q, 1, 0).astype(out.dtype)
        out[:, DH:] = dot(probs_b[n], cot, 1, 0).astype(out.dtype)
    text_key = dot(dscores[3], q, 1, 0).astype(BF)
    text_value = dot(probs_b[3], cot, 1, 0).astype(BF)
    first = (slab & 1) == 0
    keep[...] = jnp.where(first, text_key, text_value)
    swap[0, TILE:] = jnp.where(first, text_value, text_key)


def attention(sample, scalars, q, prev, own, nxt, text_k, text_v, out_grad, swap):
    kv = pl.BlockSpec((TILE, 2 * DH), lambda h: (0, h))
    tile = pl.BlockSpec((TILE, DH), lambda h: (sample, h))
    text = pl.BlockSpec((1, TEXT, DH), lambda h: (sample, 0, h))
    arrays = [*scalars, q, prev, own, nxt, text_k, text_v, out_grad]
    in_specs = [SMEM, SMEM, SMEM, tile, kv, kv, kv, text, text, tile]
    aliases = {}
    if swap is not None:
        aliases = {len(arrays): 0}
        arrays.append(swap)
        in_specs.append(pl.BlockSpec(memory_space=pl.ANY))
    return pl.pallas_call(
        functools.partial(attention_kernel, sample),
        grid=(HEADS_DEV,),
        in_specs=in_specs,
        out_specs=[
            pl.BlockSpec((1, TILE + TEXT, DH), lambda h: (sample, 0, h)),
            kv,
            kv,
            kv,
            pl.BlockSpec((TEXT, DH), lambda h: (0, h)),
        ],
        out_shape=[
            jax.ShapeDtypeStruct((SAMPLES, TILE + TEXT, CH), BF),
            jax.ShapeDtypeStruct((TILE, 2 * CH), BF),
            jax.ShapeDtypeStruct((TILE, 2 * CH), F32),
            jax.ShapeDtypeStruct((TILE, 2 * CH), BF),
            jax.ShapeDtypeStruct((TEXT, CH), BF),
        ],
        input_output_aliases=aliases,
        compiler_params=pltpu.CompilerParams(vmem_limit_bytes=12 * MIB),
        cost_estimate=COST,
        name="attention",
    )(*arrays)


def join_kernel(before, down, low, high, out):
    out[0] = before[...]
    out[1] = total(down[...], low[...], high[...])


REDUCE_ORDER = (2, 1, 3, 0)


def hidden_kernel(sample, swap, grads, w, *outs):
    kv = grads.at[sample] if len(grads.shape) == 3 else grads
    a, y, _, _, _ = place()
    keys = [kv[:, 2 * h * DH : (2 * h + 1) * DH] for h in range(HEADS_DEV)]
    vals = [kv[:, (2 * h + 1) * DH : (2 * h + 2) * DH] for h in range(HEADS_DEV)]
    g = [swap[sample, :TILE], jnp.concatenate(keys, axis=1), jnp.concatenate(vals, axis=1)]
    for n, d in enumerate(REDUCE_ORDER):
        yj = (y + d) & 3
        part = None
        for c in range(3):
            wc = jnp.concatenate([w[c, a, yj], w[c, 1 - a, yj]], axis=0)
            term = dot(g[c], wc, 1, 1)
            part = term if part is None else part + term
        if d == 2:
            outs[0][...] = part[:, :CH].astype(BF)
            outs[1][...] = part[:, CH:].astype(BF)
        else:
            outs[n + 1][0] = part[:, :CH].astype(BF)
            outs[n + 1][1] = part[:, CH:].astype(BF)


def hidden_parts(sample, swap, grads, w):
    one, two = ((TILE, CH), (2, TILE, CH))
    kernel = functools.partial(hidden_kernel, sample)
    return call(kernel, "hidden_parts", [swap, grads, w], [one, one, two, two, two], 4)


def bundle_kernel(got_same, got_flip, up, down, up_out, down_out):
    up_out[0] = up[0]
    up_out[1] = total(up[1], got_flip[...])
    down_out[0] = total(down[0], got_same[...])
    down_out[1] = down[1]


def hidden_far(far_same, far_flip, up, down, here):
    return (head_move(far_same, 0, 3), head_move(far_flip, 0, 1), up, down, here)


def hidden_sides(got_same, got_flip, up, down, here):
    two = (2, TILE, CH)
    up, down = call(
        bundle_kernel,
        "hidden_bundle",
        [got_same, got_flip, up, down],
        [two, two],
        4,
        input_output_aliases={2: 0, 3: 1},
    )
    return (here, head_move(up, 0, 1), head_move(down, 0, 3))


def across_kernel(here, up, down, out):
    out[...] = total(here[1], up[1], down[1])


def hidden_across(terms):
    return head_move(call(across_kernel, "hidden_across", terms, [(TILE, CH)], 4)[0], 1, 0)


def hidden_final_kernel(*refs):
    out = refs[-1]
    for s in range(SAMPLES):
        here, up, down, across = refs[4 * s : 4 * s + 4]
        out[s * TILE : (s + 1) * TILE] = total(here[0], up[0], down[0], across[...])


def query_weight_kernel(x_own, x_twin, own, twin, keep0, keep1, *rest):
    outs, text = (rest[:4], rest[4])
    _, _, z, _, _ = place()
    g = jnp.concatenate([r[s, :TILE] for r in (own, twin) for s in range(SAMPLES)], axis=0)
    for s, keep in enumerate((keep0, keep1)):
        both = total(keep[...], twin[s, TILE:])
        text[2 * s] = both[: TEXT // 2]
        text[2 * s + 1] = both[TEXT // 2 :]
    for d in (2, 1, 3, 0):
        j = (z + d) & 3
        x = jnp.concatenate([x_own[j], x_twin[j]], axis=0)
        outs[d][:CH] = dot(x, g, 0, 0).astype(BF)
        outs[d][CH:] = text[j]


def query_weight_parts(*arrays):
    return call(
        query_weight_kernel,
        "query_weight_parts",
        arrays,
        [(CH + TEXT // 2, CH)] * 4,
        4,
        [pltpu.VMEM((4, TEXT // 2, CH), BF)],
    )


def weight_kernel(x_own, x_twin, own, twin, *outs):
    _, _, z, _, _ = place()
    g = jnp.concatenate([r[s] for r in (own, twin) for s in range(SAMPLES)], axis=0)
    for d in (2, 1, 3, 0):
        j = (z + d) & 3
        x = jnp.concatenate([x_own[j], x_twin[j]], axis=0)
        part = dot(x, g, 0, 0).astype(BF)
        for h in range(HEADS_DEV):
            key, value = (2 * h * DH, (2 * h + 1) * DH)
            outs[d][:, h * DH : (h + 1) * DH] = part[:, key : key + DH]
            outs[d][:, CH + h * DH : CH + (h + 1) * DH] = part[:, value : value + DH]


def weight_parts(*arrays):
    return call(weight_kernel, "weight_parts", arrays, [(CH, 2 * CH)] * 4, 6)


def z_moves(parts):
    return [slab_move(parts[d], d, 0, 0) for d in (2, 1, 3)]


def weight_halves_kernel(*refs):
    query, rest, (near, far) = (refs[:4], refs[4:8], refs[8:])
    _, _, _, x, core = place()
    home = x == core
    for half in range(2):
        rows = slice(half * CH // 2, (half + 1) * CH // 2)
        q = total(*[r[rows] for r in query])
        kv = total(*[r[rows] for r in rest])
        is_far = (core == half) == home

        @pl.when(is_far)
        def _():
            far[:, :CH] = q
            far[:, CH:] = kv

        @pl.when(jnp.logical_not(is_far))
        def _():
            near[:, :CH] = q
            near[:, CH:] = kv


def weight_final_kernel(far, got_first, got_second, out):
    _, _, _, x, core = place()
    for c in range(3):
        cols = slice(c * CH, (c + 1) * CH)
        kept = jnp.where(x == core, far[:, cols], got_second[:, cols])
        out[c] = total(kept, got_first[:, cols])


def weight_home(query, rest):
    half = (CH // 2, 3 * CH)
    near, far = call(weight_halves_kernel, "weight_halves", [*query, *rest], [half, half], 6)
    first, second = ([], [])
    for s in range(16):
        z, x, c = (s // 4, s // 2 % 2, s % 2)
        if x == c:
            first.append((s, z * 4 + x * 2 + 1 - c))
        else:
            first.append((s, z * 4 + (1 - x) * 2 + c))
            second.append((s, z * 4 + (1 - x) * 2 + 1 - c))
    got_first = lax.ppermute(near, "slab", first)
    got_second = lax.ppermute(far, "slab", second)
    out = call(
        weight_final_kernel, "weight_final", [far, got_first, got_second], [(3, CH // 2, CH)], 4
    )[0]
    return jnp.transpose(out, (1, 0, 2))


def text_sum_kernel(*refs):
    refs[-1][...] = total(*[r[CH:] for r in refs[:-1]])


def text_pair_kernel(one, two, out):
    out[...] = total(one[...], two[...])


def text_full_kernel(own, far, below, above, out):
    _, _, z, _, _ = place()
    for d, ref in ((0, own), (2, far), (1, below), (3, above)):
        out[(z - d) & 3] = ref[...]


def text_final_kernel(full, twin, key, value):
    _, _, _, _, core = place()
    key[...] = jnp.where(core == 0, full[...], twin[...])
    value[...] = jnp.where(core == 0, twin[...], full[...])


def text_spread(parts):
    shape = (TEXT // 2, CH)
    quarter = call(text_sum_kernel, "text_sum", parts, [shape], 4)[0]
    pair = [quarter, slab_move(quarter, 0, 1, 0)]
    quarter = call(text_pair_kernel, "text_pair", pair, [shape], 4)[0]
    full = call(text_full_kernel, "text_full", [quarter, *z_moves([quarter] * 4)], [(4, *shape)], 4)[0]
    both = [full, slab_move(full, 0, 0, 1)]
    pair = call(text_final_kernel, "text_final", both, [(4, *shape)] * 2, 4)
    return jnp.stack([part.reshape(SAMPLES, TEXT, CH) for part in pair], axis=2)


def body(hidden, w_qkv, text_keys, text_values, text_len, advantage, out_grad, tile_lists):
    w = jnp.transpose(w_qkv, (1, 0, 2)).reshape(3, 2, 4, CH, CH)
    scalars = (tile_lists, text_len, advantage)
    q, *kvs, mine, other = project(hidden, w)
    halos = [(slab_step(kvs[0], 1), slab_step(kvs[0], -1))]
    halos, other, late = lax.optimization_barrier((halos, other, kvs[1]))
    theirs = slab_move(other, 0, 0, 1)
    halos.append((slab_step(late, 1), slab_step(late, -1)))
    ends, keeps, swap = ([], [], None)
    for s in range(SAMPLES):
        if s == 1:
            q, _, theirs = lax.optimization_barrier((q, swap, theirs))
        swap, dprev, down, dnext, keep = attention(
            s, scalars, q, halos[s][0], kvs[s], halos[s][1], text_keys, text_values, out_grad, swap
        )
        keeps.append(keep)
        ends.append((down, dnext, dprev))
    sums = [(ends[0][0], slab_step(ends[0][1], 1), slab_step(ends[0][2], -1))]
    down, dnext, dprev = ends[1]
    sums, swap, dnext, dprev = lax.optimization_barrier((sums, swap, dnext, dprev))
    sums.append((down, slab_step(dnext, 1), slab_step(dprev, -1)))
    swap_twin = slab_move(swap, 0, 0, 1)
    query = query_weight_parts(mine, theirs, swap, swap_twin, *keeps)
    grad = total(*sums[0])
    first = hidden_parts(0, swap, grad, w)
    sums[1], _ = lax.optimization_barrier((sums[1], (query, first)))
    query = [query[0], *z_moves(query)]
    first = hidden_sides(*hidden_far(*first))
    grads = call(join_kernel, "join", [grad, *sums[1]], [(SAMPLES, TILE, 2 * CH)], 4)[0]
    rest = weight_parts(mine, theirs, grads, slab_move(grads, 0, 0, 1))
    grads, rest = lax.optimization_barrier((grads, rest))
    rest = [rest[0], *z_moves(rest)]
    second = hidden_sides(*hidden_far(*hidden_parts(1, swap, grads, w)))
    text_parts, rest[2] = lax.optimization_barrier((query, rest[2]))
    ends = [*first, hidden_across(first), *second, hidden_across(second)]
    hidden_grad = call(hidden_final_kernel, "hidden_final", ends, [(ROWS, CH)], 4)[0]
    text_grad = text_spread(text_parts)
    weight_grad = weight_home(query, rest)
    return (hidden_grad, weight_grad, text_grad)


def solution(mesh):
    in_specs = (
        P("slab", "head"),
        P(None, None, "head"),
        P(None, None, "head"),
        P(None, None, "head"),
        P(),
        P(),
        P("slab", "head"),
        P("slab", None),
    )
    out_specs = (P("slab", "head"), P("slab", None, "head"), P(None, None, None, "head"))
    return jax.shard_map(body, mesh=mesh, in_specs=in_specs, out_specs=out_specs, check_vma=False)
```

```python
import functools
import math

import jax
import jax.numpy as jnp
from jax import lax
from jax.experimental import pallas as pl
from jax.experimental.pallas import tpu as pltpu
from jax.sharding import PartitionSpec as P

DH = 128
TILE = 384
SAMPLES = 2
HEADS_DEV = 3
CH = 384
TEXT = 256
BF = jnp.bfloat16
F32 = jnp.float32
SCALE = 1.0 / math.sqrt(DH)
EXP_SCALE = SCALE * math.log2(math.e)
MIB = 1024 * 1024
COST = pl.CostEstimate(flops=10**6, bytes_accessed=10**4, transcendentals=0)

VMEM = pl.BlockSpec(memory_space=pltpu.VMEM)
SMEM = pl.BlockSpec(memory_space=pltpu.SMEM)


def dot(a, b, ca, cb):
    return lax.dot_general(a, b, (((ca,), (cb,)), ((), ())), preferred_element_type=F32)


def head_move(x, dx, dy):
    pairs = [(h, ((h // 4) ^ dx) * 4 + (h + dy) % 4) for h in range(8)]
    return lax.ppermute(x, "head", pairs)


def slab_move(x, dz, dx, dc):
    pairs = [
        (s, ((s // 4 + dz) % 4) * 4 + ((s // 2 % 2) ^ dx) * 2 + ((s % 2) ^ dc)) for s in range(16)
    ]
    return lax.ppermute(x, "slab", pairs)


def slab_step(x, distance):
    pairs = [(i, (i + distance) % 16) for i in range(16)]
    return lax.ppermute(x, "slab", pairs)


def place():
    slab, head = (lax.axis_index("slab"), lax.axis_index("head"))
    return (head >> 2, head & 3, slab >> 2, (slab >> 1) & 1, slab & 1)


def call(kernel, name, arrays, shapes, limit, scratch=(), **options):
    return pl.pallas_call(
        kernel,
        in_specs=[VMEM] * len(arrays),
        out_specs=[VMEM] * len(shapes),
        out_shape=[jax.ShapeDtypeStruct(shape, BF) for shape in shapes],
        scratch_shapes=list(scratch),
        compiler_params=pltpu.CompilerParams(vmem_limit_bytes=limit * MIB),
        cost_estimate=COST,
        name=name,
        **options,
    )(*arrays)


def total(*refs):
    value = refs[0].astype(F32)
    for ref in refs[1:]:
        value = value + ref.astype(F32)
    return value.astype(BF)


ROWS = SAMPLES * TILE
FIRST = ((0, 0, 1), (3, 2, None), (1, 3, None))
SECOND = ((3, None, 0), (1, None, 1), (2, 2, None))


def load_kernel(w, out, sem):
    copy = pltpu.make_async_copy(w, out, sem)
    copy.start()
    copy.wait()


def load(w):
    return pl.pallas_call(
        load_kernel,
        in_specs=[pl.BlockSpec(memory_space=pl.ANY)],
        out_specs=VMEM,
        out_shape=jax.ShapeDtypeStruct(w.shape, BF),
        scratch_shapes=[pltpu.SemaphoreType.DMA],
        compiler_params=pltpu.CompilerParams(vmem_limit_bytes=MIB),
        cost_estimate=COST,
        name="load",
    )(w)


def place_chunk(ref, a, yj, core, mine, other):
    z = (a * 4 + yj) >> 1
    own = ((yj ^ core) & 1) == 0

    @pl.when(own)
    def _():
        mine[z] = ref[...]

    @pl.when(jnp.logical_not(own))
    def _():
        other[z] = ref[...]


def project_kernel(steps, count, *refs):
    chunks, w, rest = (refs[:count], refs[count], refs[count + 1 :])
    acc, mine, other = rest[-3:]
    start = rest[0] if len(rest) > 3 else None
    a, y, _, _, core = place()
    for n, (d, r0, r1) in enumerate(steps):
        yj = (y + d) & 3
        pair = [(r, chunks[i]) for r, i in ((a, r0), (1 - a, r1)) if i is not None]
        for r, ref in pair:
            place_chunk(ref, r, yj, core, mine, other)
        x = jnp.concatenate([ref[...] for _, ref in pair], axis=1)
        for c in range(3):
            wc = jnp.concatenate([w[c, r, yj] for r, _ in pair], axis=0)
            part = dot(x, wc, 1, 0)
            if n > 0:
                acc[c] += part
            elif start is None:
                acc[c] = part
            else:
                acc[c] = start[c] + part


def project_step(steps, chunks, w, before):
    count = len(chunks)
    return pl.pallas_call(
        functools.partial(project_kernel, steps, count),
        in_specs=[VMEM] * (count + 1 + len(before)),
        out_specs=[VMEM] * 3,
        out_shape=[
            jax.ShapeDtypeStruct((3, ROWS, CH), F32),
            jax.ShapeDtypeStruct((4, ROWS, CH), BF),
            jax.ShapeDtypeStruct((4, ROWS, CH), BF),
        ],
        input_output_aliases={count + 1 + n: n for n in range(len(before))},
        compiler_params=pltpu.CompilerParams(vmem_limit_bytes=6 * MIB),
        cost_estimate=COST,
        name="project",
    )(*chunks, w, *before)


def project_late_kernel(first, second, w, acc, mine_in, other_in, q_out, *refs):
    kv_outs, (mine, other, last) = (refs[:SAMPLES], refs[SAMPLES:])
    a, y, _, _, core = place()
    yj = (y + 2) & 3
    last[:TILE] = first[...]
    last[TILE:] = second[...]
    place_chunk(last, 1 - a, yj, core, mine, other)
    for c in (1, 2, 0):
        part = (acc[c] + dot(last[...], w[c, 1 - a, yj], 1, 0)).astype(BF)
        if c == 0:
            q_out[...] = part
            continue
        for s, kv_out in enumerate(kv_outs):
            for h in range(HEADS_DEV):
                at = (2 * h + c - 1) * DH
                kv_out[:, at : at + DH] = part[s * TILE : (s + 1) * TILE, h * DH : (h + 1) * DH]


def project(hidden, w):
    flip = head_move(hidden, 1, 0)
    below = head_move(hidden, 0, 1)
    above = head_move(hidden, 0, 3)
    flip, below, above, w = lax.optimization_barrier((flip, below, above, load(w)))
    flip_below = head_move(below, 1, 0)
    flip_above = head_move(flip, 0, 3)
    far = head_move(below, 0, 1)
    sums = project_step(FIRST, [hidden, flip, below, above], w, [])
    late = [flip_below, flip_above, far]
    late, sums = lax.optimization_barrier((late, sums))
    last = [head_move(late[0][:TILE], 0, 1), head_move(late[1][TILE:], 0, 3)]
    acc, mine, other = project_step(SECOND, late, w, sums)
    shapes = [(ROWS, CH), (TILE, 2 * CH), (TILE, 2 * CH), (4, ROWS, CH), (4, ROWS, CH)]
    outs = call(
        project_late_kernel,
        "project_late",
        [*last, w, acc, mine, other],
        shapes,
        6,
        [pltpu.VMEM((ROWS, CH), BF)],
        input_output_aliases={4: 3, 5: 4},
    )
    return (w, *outs)


def attention_kernel(
    sample,
    lists,
    lengths,
    adv,
    q_ref,
    prev,
    own,
    nxt,
    tk_ref,
    tv_ref,
    og_ref,
    *refs,
):
    swap, dprev, down, dnext, keep = refs[-5:]
    slab = lax.axis_index("slab")
    tile = slab * SAMPLES + sample
    before, after = (False, False)
    for n in range(lists.shape[1]):
        before = before | (lists[sample, n] == tile - SAMPLES)
        after = after | (lists[sample, n] == tile + SAMPLES)
    before = before & (slab > 0)
    q = q_ref[...]
    cot = (adv[sample] * og_ref[...].astype(F32)).astype(BF)
    rows = lax.broadcasted_iota(jnp.int32, (TEXT, TILE), 0)
    live = rows < lengths[sample]
    keys = [prev[:, :DH], own[:, :DH], nxt[:, :DH], tk_ref[0]]
    vals = [prev[:, DH:], own[:, DH:], nxt[:, DH:], tv_ref[0]]
    scores = [dot(k, q, 1, 1) for k in keys]
    scores[0] = jnp.where(before, scores[0], -jnp.inf)
    scores[2] = jnp.where(after, scores[2], -jnp.inf)
    scores[3] = jnp.where(live, scores[3], -jnp.inf)
    top = jnp.max(scores[1], axis=0, keepdims=True)
    for n in (0, 2, 3):
        top = jnp.maximum(top, jnp.max(scores[n], axis=0, keepdims=True))
    powers = [jnp.exp2((s - top) * EXP_SCALE) for s in scores]
    total = sum(jnp.sum(p, axis=0, keepdims=True) for p in powers)
    inverse = 1.0 / total
    probs = [p * inverse for p in powers]
    probs_b = [p.astype(BF) for p in probs]
    dprobs = [dot(v, cot, 1, 1) for v in vals]
    delta = sum(
        jnp.sum(p.astype(F32) * d, axis=0, keepdims=True) for p, d in zip(probs_b, dprobs)
    )
    dscores = [(p * (d - delta) * SCALE).astype(BF) for p, d in zip(probs, dprobs)]
    grad = dot(keys[0], dscores[0], 0, 0)
    for n in (1, 2, 3):
        grad += dot(keys[n], dscores[n], 0, 0)
    swap[0, :TILE] = grad.T.astype(BF)
    for n, out in ((0, dprev), (1, down), (2, dnext)):
        out[:, :DH] = dot(dscores[n], q, 1, 0).astype(out.dtype)
        out[:, DH:] = dot(probs_b[n], cot, 1, 0).astype(out.dtype)
    text_key = dot(dscores[3], q, 1, 0).astype(BF)
    text_value = dot(probs_b[3], cot, 1, 0).astype(BF)
    first = (slab & 1) == 0
    keep[...] = jnp.where(first, text_key, text_value)
    swap[0, TILE:] = jnp.where(first, text_value, text_key)


def attention(sample, scalars, q, prev, own, nxt, text_k, text_v, out_grad, swap):
    kv = pl.BlockSpec((TILE, 2 * DH), lambda h: (0, h))
    tile = pl.BlockSpec((TILE, DH), lambda h: (sample, h))
    text = pl.BlockSpec((1, TEXT, DH), lambda h: (sample, 0, h))
    arrays = [*scalars, q, prev, own, nxt, text_k, text_v, out_grad]
    in_specs = [SMEM, SMEM, SMEM, tile, kv, kv, kv, text, text, tile]
    aliases = {}
    if swap is not None:
        aliases = {len(arrays): 0}
        arrays.append(swap)
        in_specs.append(pl.BlockSpec(memory_space=pl.ANY))
    return pl.pallas_call(
        functools.partial(attention_kernel, sample),
        grid=(HEADS_DEV,),
        in_specs=in_specs,
        out_specs=[
            pl.BlockSpec((1, TILE + TEXT, DH), lambda h: (sample, 0, h)),
            kv,
            kv,
            kv,
            pl.BlockSpec((TEXT, DH), lambda h: (0, h)),
        ],
        out_shape=[
            jax.ShapeDtypeStruct((SAMPLES, TILE + TEXT, CH), BF),
            jax.ShapeDtypeStruct((TILE, 2 * CH), BF),
            jax.ShapeDtypeStruct((TILE, 2 * CH), F32),
            jax.ShapeDtypeStruct((TILE, 2 * CH), BF),
            jax.ShapeDtypeStruct((TEXT, CH), BF),
        ],
        input_output_aliases=aliases,
        compiler_params=pltpu.CompilerParams(vmem_limit_bytes=12 * MIB),
        cost_estimate=COST,
        name="attention",
    )(*arrays)


def join_kernel(before, down, low, high, out):
    out[0] = before[...]
    out[1] = total(down[...], low[...], high[...])


REDUCE = ((2, "far", "flip_far"), (3, "below", "flip_below"), (1, "above", "flip_above"), (0, "own", "flip"))
PARTS = ("flip_far", "far", "below", "flip_below", "above", "flip_above", "own", "flip")


def hidden_kernel(sample, swap, grads, w, *refs):
    outs = dict(zip(PARTS, refs[-len(PARTS) :], strict=True))
    kv = grads.at[sample] if len(grads.shape) == 3 else grads
    rows = slice(sample * TILE, (sample + 1) * TILE)
    a, y, _, _, _ = place()
    keys = [kv[:, 2 * h * DH : (2 * h + 1) * DH] for h in range(HEADS_DEV)]
    vals = [kv[:, (2 * h + 1) * DH : (2 * h + 2) * DH] for h in range(HEADS_DEV)]
    g = [swap[sample, :TILE], jnp.concatenate(keys, axis=1), jnp.concatenate(vals, axis=1)]
    for d, same, flip in REDUCE:
        yj = (y + d) & 3
        part = None
        for c in range(3):
            wc = jnp.concatenate([w[c, a, yj], w[c, 1 - a, yj]], axis=0)
            term = dot(g[c], wc, 1, 1)
            part = term if part is None else part + term
        outs[same][rows] = part[:, :CH].astype(BF)
        outs[flip][... if flip == "flip_far" else rows] = part[:, CH:].astype(BF)


def hidden_parts(sample, swap, grads, w, before):
    shapes = [(TILE, CH)] + [(ROWS, CH)] * (len(PARTS) - 1)
    arrays = [swap, grads, w, *before]
    return call(
        functools.partial(hidden_kernel, sample),
        "hidden_parts",
        arrays,
        shapes,
        4,
        input_output_aliases={3 + n: 1 + n for n in range(len(before))},
    )


def far_kernel(below, above, got_below, got_above, below_out, above_out):
    below_out[:TILE] = total(below[:TILE], got_below[...])
    below_out[TILE:] = below[TILE:]
    above_out[:TILE] = above[:TILE]
    above_out[TILE:] = total(above[TILE:], got_above[...])


def near_kernel(below, flip, got_flip_below, got_far, got_flip_above, below_out, flip_out):
    below_out[...] = total(below[...], got_flip_below[...], got_far[...])
    flip_out[...] = total(flip[...], got_flip_above[...])


def sum_kernel(*refs):
    refs[-1][...] = total(*[r[...] for r in refs[:-1]])


def hidden_reduce(farthest, parts):
    part = dict(zip(PARTS[1:], parts, strict=True))
    both = [(ROWS, CH)] * 2
    got = [head_move(farthest[0], 0, 3), head_move(farthest[1], 0, 1)]
    sides = [part["flip_below"], part["flip_above"], *got]
    flip_below, flip_above = call(
        far_kernel, "hidden_far", sides, both, 4, input_output_aliases={0: 0, 1: 1}
    )
    got = [head_move(flip_below, 1, 0), head_move(part["far"], 0, 3), head_move(flip_above, 0, 1)]
    sides = [part["below"], part["flip"], *got]
    below, flip = call(
        near_kernel, "hidden_near", sides, both, 4, input_output_aliases={0: 0, 1: 1}
    )
    got = [head_move(below, 0, 3), head_move(part["above"], 0, 1), head_move(flip, 1, 0)]
    return call(sum_kernel, "hidden_sum", [part["own"], *got], both[:1], 4)[0]


RING = [(CH // 2, 3 * CH)] * 2 + [(CH, 3 * CH)] * 3


def ring_store(outs, n, cols, part):
    if n == 0:
        outs[0][:, cols] = part[: CH // 2]
        outs[1][:, cols] = part[CH // 2 :]
    else:
        outs[n + 1][:, cols] = part


def query_weight_kernel(x_own, x_twin, own, twin, keep0, keep1, *outs):
    _, _, z, _, _ = place()
    g = jnp.concatenate([r[s, :TILE] for r in (own, twin) for s in range(SAMPLES)], axis=0)
    for s, keep in enumerate((keep0, keep1)):
        outs[5][s] = total(keep[...], twin[s, TILE:])
    for n, d in enumerate((2, 1, 3, 0)):
        j = (z + d) & 3
        x = jnp.concatenate([x_own[j], x_twin[j]], axis=0)
        ring_store(outs, n, slice(0, CH), dot(x, g, 0, 0).astype(BF))


def query_weight_parts(*arrays):
    shapes = [*RING, (SAMPLES, TEXT, CH)]
    return call(query_weight_kernel, "query_weight_parts", arrays, shapes, 4)


def weight_kernel(x_own, x_twin, own, twin, *refs):
    outs = refs[len(RING) :]
    _, _, z, _, _ = place()
    g = jnp.concatenate([r[s] for r in (own, twin) for s in range(SAMPLES)], axis=0)
    for n, d in enumerate((2, 1, 3, 0)):
        j = (z + d) & 3
        x = jnp.concatenate([x_own[j], x_twin[j]], axis=0)
        part = dot(x, g, 0, 0).astype(BF)
        for h in range(HEADS_DEV):
            for k in range(2):
                at, to = ((2 * h + k) * DH, (k + 1) * CH + h * DH)
                ring_store(outs, n, slice(to, to + DH), part[:, at : at + DH])


def weight_parts(arrays, before):
    aliases = {len(arrays) + n: n for n in range(len(RING))}
    arrays = [*arrays, *before]
    return call(weight_kernel, "weight_parts", arrays, RING, 6, input_output_aliases=aliases)


def weight_far_kernel(up, down, got_up, got_down, up_out, down_out):
    half = CH // 2
    up_out[:half] = total(up[:half], got_up[...])
    up_out[half:] = up[half:]
    down_out[:half] = down[:half]
    down_out[half:] = total(down[half:], got_down[...])


def weight_ring(far_up, far_down, up, down, own):
    got = [slab_move(far_up, 1, 0, 0), slab_move(far_down, 3, 0, 0)]
    both = RING[3:]
    up, down = call(
        weight_far_kernel, "weight_far", [up, down, *got], both, 4, input_output_aliases={0: 0, 1: 1}
    )
    return [own, slab_move(up, 1, 0, 0), slab_move(down, 3, 0, 0)]


def weight_halves_kernel(own, up, down, near, far):
    _, _, _, x, core = place()
    home = x == core
    for half in range(2):
        rows = slice(half * CH // 2, (half + 1) * CH // 2)
        part = total(own[rows], up[rows], down[rows])
        is_far = (core == half) == home

        @pl.when(is_far)
        def _():
            far[...] = part

        @pl.when(jnp.logical_not(is_far))
        def _():
            near[...] = part


def weight_final_kernel(far, got_first, got_second, out):
    _, _, _, x, core = place()
    for c in range(3):
        cols = slice(c * CH, (c + 1) * CH)
        kept = jnp.where(x == core, far[:, cols], got_second[:, cols])
        out[c] = total(kept, got_first[:, cols])


def weight_home(parts):
    half = (CH // 2, 3 * CH)
    near, far = call(weight_halves_kernel, "weight_halves", parts, [half, half], 6)
    first, second = ([], [])
    for s in range(16):
        z, x, c = (s // 4, s // 2 % 2, s % 2)
        if x == c:
            first.append((s, z * 4 + x * 2 + 1 - c))
        else:
            first.append((s, z * 4 + (1 - x) * 2 + c))
            second.append((s, z * 4 + (1 - x) * 2 + 1 - c))
    got_first = lax.ppermute(near, "slab", first)
    got_second = lax.ppermute(far, "slab", second)
    out = call(
        weight_final_kernel, "weight_final", [far, got_first, got_second], [(3, CH // 2, CH)], 4
    )[0]
    return jnp.transpose(out, (1, 0, 2))


def text_final_kernel(full, twin, key, value):
    _, _, _, _, core = place()
    key[...] = jnp.where(core == 0, full[...], twin[...])
    value[...] = jnp.where(core == 0, twin[...], full[...])


def text_spread(part):
    shape = (SAMPLES, TEXT, CH)
    for bit in (4, 8, 2):
        got = lax.ppermute(part, "slab", [(s, s ^ bit) for s in range(16)])
        part = call(sum_kernel, "text_pair", [part, got], [shape], 4)[0]
    pair = call(text_final_kernel, "text_final", [part, slab_move(part, 0, 0, 1)], [shape] * 2, 4)
    return jnp.stack(pair, axis=2)


def body(hidden, w_qkv, text_keys, text_values, text_len, advantage, out_grad, tile_lists):
    w = jnp.transpose(w_qkv, (1, 0, 2)).reshape(3, 2, 4, CH, CH)
    scalars = (tile_lists, text_len, advantage)
    w, q, *kvs, mine, other = project(hidden, w)
    halos = [(slab_step(kvs[0], 1), slab_step(kvs[0], -1))]
    halos, other, late = lax.optimization_barrier((halos, other, kvs[1]))
    theirs = slab_move(other, 0, 0, 1)
    halos.append((slab_step(late, 1), slab_step(late, -1)))
    ends, keeps, swap = ([], [], None)
    for s in range(SAMPLES):
        if s == 1:
            q, _, theirs = lax.optimization_barrier((q, swap, theirs))
        swap, dprev, down, dnext, keep = attention(
            s, scalars, q, halos[s][0], kvs[s], halos[s][1], text_keys, text_values, out_grad, swap
        )
        keeps.append(keep)
        ends.append((down, dnext, dprev))
    sums = [(ends[0][0], slab_step(ends[0][1], 1), slab_step(ends[0][2], -1))]
    down, dnext, dprev = ends[1]
    sums, dnext, dprev = lax.optimization_barrier((sums, dnext, dprev))
    sums.append((down, slab_step(dnext, 1), slab_step(dprev, -1)))
    swap_twin = slab_move(swap, 0, 0, 1)
    *query, text = query_weight_parts(mine, theirs, swap, swap_twin, *keeps)
    grad, _ = lax.optimization_barrier((total(*sums[0]), text))
    far, *parts = hidden_parts(0, swap, grad, w, [])
    sums[1], _ = lax.optimization_barrier((sums[1], parts))
    grads = call(join_kernel, "join", [grad, *sums[1]], [(SAMPLES, TILE, 2 * CH)], 4)[0]
    twin = slab_move(grads, 0, 0, 1)
    last, *parts = hidden_parts(1, swap, grads, w, parts)
    rest = weight_parts([mine, theirs, grads, twin], query)
    hidden_grad = hidden_reduce((far, last), parts)
    text_grad = text_spread(text)
    weight_grad = weight_home(weight_ring(*rest))
    return (hidden_grad, weight_grad, text_grad)


def solution(mesh):
    in_specs = (
        P("slab", "head"),
        P(None, None, "head"),
        P(None, None, "head"),
        P(None, None, "head"),
        P(),
        P(),
        P("slab", "head"),
        P("slab", None),
    )
    out_specs = (P("slab", "head"), P("slab", None, "head"), P(None, None, None, "head"))
    return jax.shard_map(body, mesh=mesh, in_specs=in_specs, out_specs=out_specs, check_vma=False)
```

```python
import functools
import math

import jax
import jax.numpy as jnp
from jax import lax
from jax.experimental import pallas as pl
from jax.experimental.pallas import tpu as pltpu
from jax.sharding import PartitionSpec as P

DH = 128
TILE = 384
SAMPLES = 2
HEADS_DEV = 3
CH = 384
TEXT = 256
BF = jnp.bfloat16
F32 = jnp.float32
SCALE = 1.0 / math.sqrt(DH)
EXP_SCALE = SCALE * math.log2(math.e)
MIB = 1024 * 1024
TIMES = {'load': 9.0, 'project': 14.4, 'project_late': 4.8, 'attention': 24.6, 'join': 2.1, 'hidden_parts': 11.7, 'query_weight_parts': 8.25, 'weight_parts': 11.4, 'hidden_far': 1.35, 'hidden_near': 3.45, 'hidden_sum': 3.3, 'weight_far': 1.95, 'weight_halves': 1.8, 'weight_final': 2.7, 'text_pair': 1.5, 'text_final': 1.5}


def cost(name):
    return pl.CostEstimate(flops=int(TIMES[name] * 1.15e9), bytes_accessed=10**4, transcendentals=0)

VMEM = pl.BlockSpec(memory_space=pltpu.VMEM)
SMEM = pl.BlockSpec(memory_space=pltpu.SMEM)


def dot(a, b, ca, cb):
    return lax.dot_general(a, b, (((ca,), (cb,)), ((), ())), preferred_element_type=F32)


def head_move(x, dx, dy):
    pairs = [(h, ((h // 4) ^ dx) * 4 + (h + dy) % 4) for h in range(8)]
    return lax.ppermute(x, "head", pairs)


def slab_move(x, dz, dx, dc):
    pairs = [
        (s, ((s // 4 + dz) % 4) * 4 + ((s // 2 % 2) ^ dx) * 2 + ((s % 2) ^ dc)) for s in range(16)
    ]
    return lax.ppermute(x, "slab", pairs)


def slab_step(x, distance):
    pairs = [(i, (i + distance) % 16) for i in range(16)]
    return lax.ppermute(x, "slab", pairs)


def place():
    slab, head = (lax.axis_index("slab"), lax.axis_index("head"))
    return (head >> 2, head & 3, slab >> 2, (slab >> 1) & 1, slab & 1)


def call(kernel, name, arrays, shapes, limit, scratch=(), **options):
    return pl.pallas_call(
        kernel,
        in_specs=[VMEM] * len(arrays),
        out_specs=[VMEM] * len(shapes),
        out_shape=[jax.ShapeDtypeStruct(shape, BF) for shape in shapes],
        scratch_shapes=list(scratch),
        compiler_params=pltpu.CompilerParams(vmem_limit_bytes=limit * MIB),
        cost_estimate=cost(name),
        name=name,
        **options,
    )(*arrays)


def total(*refs):
    value = refs[0].astype(F32)
    for ref in refs[1:]:
        value = value + ref.astype(F32)
    return value.astype(BF)


ROWS = SAMPLES * TILE
FIRST = ((0, 0, 1), (3, 2, None), (1, 3, None))
SECOND = ((3, None, 0), (1, None, 1), (2, 2, None))


def load_kernel(w, out, sem):
    copy = pltpu.make_async_copy(w, out, sem)
    copy.start()
    copy.wait()


def load(w):
    return pl.pallas_call(
        load_kernel,
        in_specs=[pl.BlockSpec(memory_space=pl.ANY)],
        out_specs=VMEM,
        out_shape=jax.ShapeDtypeStruct(w.shape, BF),
        scratch_shapes=[pltpu.SemaphoreType.DMA],
        compiler_params=pltpu.CompilerParams(vmem_limit_bytes=MIB),
        cost_estimate=cost("load"),
        name="load",
    )(w)


def place_chunk(ref, a, yj, core, mine, other):
    z = (a * 4 + yj) >> 1
    own = ((yj ^ core) & 1) == 0

    @pl.when(own)
    def _():
        mine[z] = ref[...]

    @pl.when(jnp.logical_not(own))
    def _():
        other[z] = ref[...]


def project_kernel(steps, count, *refs):
    chunks, w, rest = (refs[:count], refs[count], refs[count + 1 :])
    acc, mine, other = rest[-3:]
    start = rest[0] if len(rest) > 3 else None
    a, y, _, _, core = place()
    for n, (d, r0, r1) in enumerate(steps):
        yj = (y + d) & 3
        pair = [(r, chunks[i]) for r, i in ((a, r0), (1 - a, r1)) if i is not None]
        for r, ref in pair:
            place_chunk(ref, r, yj, core, mine, other)
        x = jnp.concatenate([ref[...] for _, ref in pair], axis=1)
        for c in range(3):
            wc = jnp.concatenate([w[c, r, yj] for r, _ in pair], axis=0)
            part = dot(x, wc, 1, 0)
            if n > 0:
                acc[c] += part
            elif start is None:
                acc[c] = part
            else:
                acc[c] = start[c] + part


def project_step(steps, chunks, w, before):
    count = len(chunks)
    return pl.pallas_call(
        functools.partial(project_kernel, steps, count),
        in_specs=[VMEM] * (count + 1 + len(before)),
        out_specs=[VMEM] * 3,
        out_shape=[
            jax.ShapeDtypeStruct((3, ROWS, CH), F32),
            jax.ShapeDtypeStruct((4, ROWS, CH), BF),
            jax.ShapeDtypeStruct((4, ROWS, CH), BF),
        ],
        input_output_aliases={count + 1 + n: n for n in range(len(before))},
        compiler_params=pltpu.CompilerParams(vmem_limit_bytes=6 * MIB),
        cost_estimate=cost("project"),
        name="project",
    )(*chunks, w, *before)


def project_late_kernel(first, second, w, acc, mine_in, other_in, q_out, *refs):
    kv_outs, (mine, other, last) = (refs[:SAMPLES], refs[SAMPLES:])
    a, y, _, _, core = place()
    yj = (y + 2) & 3
    last[:TILE] = first[...]
    last[TILE:] = second[...]
    place_chunk(last, 1 - a, yj, core, mine, other)
    for c in (1, 2, 0):
        part = (acc[c] + dot(last[...], w[c, 1 - a, yj], 1, 0)).astype(BF)
        if c == 0:
            q_out[...] = part
            continue
        for s, kv_out in enumerate(kv_outs):
            for h in range(HEADS_DEV):
                at = (2 * h + c - 1) * DH
                kv_out[:, at : at + DH] = part[s * TILE : (s + 1) * TILE, h * DH : (h + 1) * DH]


def project(hidden, w):
    flip = head_move(hidden, 1, 0)
    below = head_move(hidden, 0, 1)
    above = head_move(hidden, 0, 3)
    flip, below, above, w = lax.optimization_barrier((flip, below, above, load(w)))
    flip_below = head_move(below, 1, 0)
    flip_above = head_move(flip, 0, 3)
    far = head_move(below, 0, 1)
    sums = project_step(FIRST, [hidden, flip, below, above], w, [])
    late = [flip_below, flip_above, far]
    late, sums = lax.optimization_barrier((late, sums))
    last = [head_move(late[0][:TILE], 0, 1), head_move(late[1][TILE:], 0, 3)]
    acc, mine, other = project_step(SECOND, late, w, sums)
    shapes = [(ROWS, CH), (TILE, 2 * CH), (TILE, 2 * CH), (4, ROWS, CH), (4, ROWS, CH)]
    outs = call(
        project_late_kernel,
        "project_late",
        [*last, w, acc, mine, other],
        shapes,
        6,
        [pltpu.VMEM((ROWS, CH), BF)],
        input_output_aliases={4: 3, 5: 4},
    )
    return (w, *outs)


def attention_kernel(
    sample,
    lists,
    lengths,
    adv,
    q_ref,
    prev,
    own,
    nxt,
    tk_ref,
    tv_ref,
    og_ref,
    *refs,
):
    swap, dprev, down, dnext, keep = refs[-5:]
    slab = lax.axis_index("slab")
    tile = slab * SAMPLES + sample
    before, after = (False, False)
    for n in range(lists.shape[1]):
        before = before | (lists[sample, n] == tile - SAMPLES)
        after = after | (lists[sample, n] == tile + SAMPLES)
    before = before & (slab > 0)
    q = q_ref[...]
    cot = (adv[sample] * og_ref[...].astype(F32)).astype(BF)
    rows = lax.broadcasted_iota(jnp.int32, (TEXT, TILE), 0)
    live = rows < lengths[sample]
    keys = [prev[:, :DH], own[:, :DH], nxt[:, :DH], tk_ref[0]]
    vals = [prev[:, DH:], own[:, DH:], nxt[:, DH:], tv_ref[0]]
    scores = [dot(k, q, 1, 1) for k in keys]
    scores[0] = jnp.where(before, scores[0], -jnp.inf)
    scores[2] = jnp.where(after, scores[2], -jnp.inf)
    scores[3] = jnp.where(live, scores[3], -jnp.inf)
    top = jnp.max(scores[1], axis=0, keepdims=True)
    for n in (0, 2, 3):
        top = jnp.maximum(top, jnp.max(scores[n], axis=0, keepdims=True))
    powers = [jnp.exp2((s - top) * EXP_SCALE) for s in scores]
    total = sum(jnp.sum(p, axis=0, keepdims=True) for p in powers)
    inverse = 1.0 / total
    probs = [p * inverse for p in powers]
    probs_b = [p.astype(BF) for p in probs]
    dprobs = [dot(v, cot, 1, 1) for v in vals]
    delta = sum(
        jnp.sum(p.astype(F32) * d, axis=0, keepdims=True) for p, d in zip(probs_b, dprobs)
    )
    dscores = [(p * (d - delta) * SCALE).astype(BF) for p, d in zip(probs, dprobs)]
    grad = dot(keys[0], dscores[0], 0, 0)
    for n in (1, 2, 3):
        grad += dot(keys[n], dscores[n], 0, 0)
    swap[0, :TILE] = grad.T.astype(BF)
    for n, out in ((0, dprev), (1, down), (2, dnext)):
        out[:, :DH] = dot(dscores[n], q, 1, 0).astype(out.dtype)
        out[:, DH:] = dot(probs_b[n], cot, 1, 0).astype(out.dtype)
    text_key = dot(dscores[3], q, 1, 0).astype(BF)
    text_value = dot(probs_b[3], cot, 1, 0).astype(BF)
    first = (slab & 1) == 0
    keep[...] = jnp.where(first, text_key, text_value)
    swap[0, TILE:] = jnp.where(first, text_value, text_key)


def attention(sample, scalars, q, prev, own, nxt, text_k, text_v, out_grad, swap):
    kv = pl.BlockSpec((TILE, 2 * DH), lambda h: (0, h))
    tile = pl.BlockSpec((TILE, DH), lambda h: (sample, h))
    text = pl.BlockSpec((1, TEXT, DH), lambda h: (sample, 0, h))
    arrays = [*scalars, q, prev, own, nxt, text_k, text_v, out_grad]
    in_specs = [SMEM, SMEM, SMEM, tile, kv, kv, kv, text, text, tile]
    aliases = {}
    if swap is not None:
        aliases = {len(arrays): 0}
        arrays.append(swap)
        in_specs.append(pl.BlockSpec(memory_space=pl.ANY))
    return pl.pallas_call(
        functools.partial(attention_kernel, sample),
        grid=(HEADS_DEV,),
        in_specs=in_specs,
        out_specs=[
            pl.BlockSpec((1, TILE + TEXT, DH), lambda h: (sample, 0, h)),
            kv,
            kv,
            kv,
            pl.BlockSpec((TEXT, DH), lambda h: (0, h)),
        ],
        out_shape=[
            jax.ShapeDtypeStruct((SAMPLES, TILE + TEXT, CH), BF),
            jax.ShapeDtypeStruct((TILE, 2 * CH), BF),
            jax.ShapeDtypeStruct((TILE, 2 * CH), F32),
            jax.ShapeDtypeStruct((TILE, 2 * CH), BF),
            jax.ShapeDtypeStruct((TEXT, CH), BF),
        ],
        input_output_aliases=aliases,
        compiler_params=pltpu.CompilerParams(vmem_limit_bytes=12 * MIB),
        cost_estimate=cost("attention"),
        name="attention",
    )(*arrays)


def join_kernel(before, down, low, high, out):
    out[0] = before[...]
    out[1] = total(down[...], low[...], high[...])


REDUCE = ((2, "far", "flip_far"), (3, "below", "flip_below"), (1, "above", "flip_above"), (0, "own", "flip"))
PARTS = ("below", "flip_below", "above", "flip_above", "own", "flip")


def hidden_kernel(sample, swap, grads, w, *refs):
    outs = dict(zip(PARTS, refs[-len(PARTS) :], strict=True))
    ends = refs[-len(PARTS) - 1 - sample : -len(PARTS)]
    kv = grads.at[sample] if len(grads.shape) == 3 else grads
    rows = slice(sample * TILE, (sample + 1) * TILE)
    a, y, _, _, _ = place()
    keys = [kv[:, 2 * h * DH : (2 * h + 1) * DH] for h in range(HEADS_DEV)]
    vals = [kv[:, (2 * h + 1) * DH : (2 * h + 2) * DH] for h in range(HEADS_DEV)]
    g = [swap[sample, :TILE], jnp.concatenate(keys, axis=1), jnp.concatenate(vals, axis=1)]
    for d, same, flip in REDUCE:
        yj = (y + d) & 3
        part = None
        for c in range(3):
            wc = jnp.concatenate([w[c, a, yj], w[c, 1 - a, yj]], axis=0)
            term = dot(g[c], wc, 1, 1)
            part = term if part is None else part + term
        part = part.astype(BF)
        if d != 2:
            outs[same][rows] = part[:, :CH]
            outs[flip][rows] = part[:, CH:]
        elif sample == 0:
            ends[0][:TILE] = part[:, CH:]
            ends[0][TILE:] = part[:, :CH]
        else:
            ends[0][...] = part[:, CH:]
            ends[1][...] = part[:, :CH]


def hidden_parts(sample, swap, grads, w, before):
    ends = [(ROWS, CH)] if sample == 0 else [(TILE, CH)] * 2
    arrays = [swap, grads, w, *before]
    return call(
        functools.partial(hidden_kernel, sample),
        "hidden_parts",
        arrays,
        ends + [(ROWS, CH)] * len(PARTS),
        4,
        input_output_aliases={3 + n: len(ends) + n for n in range(len(before))},
    )


def far_kernel(below, above, got_below, got_above, below_out, above_out):
    below_out[:TILE] = total(below[:TILE], got_below[:TILE])
    below_out[TILE:] = below[TILE:]
    above_out[:TILE] = above[:TILE]
    above_out[TILE:] = total(above[TILE:], got_above[...])


def near_kernel(below, flip, flip_below, flip_above, first, second, below_out, flip_out):
    below_out[:TILE] = total(below[:TILE], flip_below[:TILE], first[TILE:])
    below_out[TILE:] = total(below[TILE:], flip_below[TILE:], second[...])
    flip_out[...] = total(flip[...], flip_above[...])


def sum_kernel(*refs):
    refs[-1][...] = total(*[r[...] for r in refs[:-1]])


def hidden_reduce(first, got_flip, got_same, parts, text):
    part = dict(zip(PARTS, parts, strict=True))
    both = [(ROWS, CH)] * 2
    sides = [part["flip_below"], part["flip_above"], first, got_flip]
    flip_below, flip_above = call(
        far_kernel, "hidden_far", sides, both, 4, input_output_aliases={0: 0, 1: 1}
    )
    got = [head_move(flip_below, 1, 0), head_move(flip_above, 0, 1)]
    sides = [part["below"], part["flip"], *got, first, got_same]
    below, flip = call(
        near_kernel, "hidden_near", sides, both, 4, input_output_aliases={0: 0, 1: 1}
    )
    got = [head_move(below, 0, 3), head_move(part["above"], 0, 1), head_move(flip, 1, 0)]
    return (call(sum_kernel, "hidden_sum", [part["own"], *got], both[:1], 4)[0], text)


RING = [(CH // 2, 3 * CH)] * 2 + [(CH, 3 * CH)] * 3


def ring_store(outs, n, cols, part):
    if n == 0:
        outs[0][:, cols] = part[: CH // 2]
        outs[1][:, cols] = part[CH // 2 :]
    else:
        outs[n + 1][:, cols] = part


def query_weight_kernel(x_own, x_twin, own, twin, keep0, keep1, *outs):
    _, _, z, _, _ = place()
    g = jnp.concatenate([r[s, :TILE] for r in (own, twin) for s in range(SAMPLES)], axis=0)
    for s, keep in enumerate((keep0, keep1)):
        outs[5][s] = total(keep[...], twin[s, TILE:])
    for n, d in enumerate((2, 1, 3, 0)):
        j = (z + d) & 3
        x = jnp.concatenate([x_own[j], x_twin[j]], axis=0)
        ring_store(outs, n, slice(0, CH), dot(x, g, 0, 0).astype(BF))


def query_weight_parts(*arrays):
    shapes = [*RING, (SAMPLES, TEXT, CH)]
    return call(query_weight_kernel, "query_weight_parts", arrays, shapes, 4)


def weight_kernel(x_own, x_twin, own, twin, *refs):
    outs = refs[len(RING) :]
    _, _, z, _, _ = place()
    g = jnp.concatenate([r[s] for r in (own, twin) for s in range(SAMPLES)], axis=0)
    for n, d in enumerate((2, 1, 3, 0)):
        j = (z + d) & 3
        x = jnp.concatenate([x_own[j], x_twin[j]], axis=0)
        part = dot(x, g, 0, 0).astype(BF)
        for h in range(HEADS_DEV):
            for k in range(2):
                at, to = ((2 * h + k) * DH, (k + 1) * CH + h * DH)
                ring_store(outs, n, slice(to, to + DH), part[:, at : at + DH])


def weight_parts(arrays, before):
    aliases = {len(arrays) + n: n for n in range(len(RING))}
    arrays = [*arrays, *before]
    return call(weight_kernel, "weight_parts", arrays, RING, 6, input_output_aliases=aliases)


def weight_far_kernel(up, down, got_up, got_down, up_out, down_out):
    half = CH // 2
    up_out[:half] = total(up[:half], got_up[...])
    up_out[half:] = up[half:]
    down_out[:half] = down[:half]
    down_out[half:] = total(down[half:], got_down[...])


def weight_ring(text, far_up, far_down, up, down, own):
    got = [slab_move(far_up, 1, 0, 0), slab_move(far_down, 3, 0, 0)]
    got, text = lax.optimization_barrier((got, text))
    both = RING[3:]
    up, down = call(
        weight_far_kernel, "weight_far", [up, down, *got], both, 4, input_output_aliases={0: 0, 1: 1}
    )
    return ([own, slab_move(up, 1, 0, 0), slab_move(down, 3, 0, 0)], text)


def weight_halves_kernel(own, up, down, near, far):
    _, _, _, x, core = place()
    home = x == core
    for half in range(2):
        rows = slice(half * CH // 2, (half + 1) * CH // 2)
        part = total(own[rows], up[rows], down[rows])
        is_far = (core == half) == home

        @pl.when(is_far)
        def _():
            far[...] = part

        @pl.when(jnp.logical_not(is_far))
        def _():
            near[...] = part


def weight_final_kernel(far, got_first, got_second, out):
    _, _, _, x, core = place()
    for c in range(3):
        cols = slice(c * CH, (c + 1) * CH)
        kept = jnp.where(x == core, far[:, cols], got_second[:, cols])
        out[c] = total(kept, got_first[:, cols])


def weight_home(parts):
    half = (CH // 2, 3 * CH)
    near, far = call(weight_halves_kernel, "weight_halves", parts, [half, half], 6)
    first, second = ([], [])
    for s in range(16):
        z, x, c = (s // 4, s // 2 % 2, s % 2)
        if x == c:
            first.append((s, z * 4 + x * 2 + 1 - c))
        else:
            first.append((s, z * 4 + (1 - x) * 2 + c))
            second.append((s, z * 4 + (1 - x) * 2 + 1 - c))
    got_first = lax.ppermute(near, "slab", first)
    got_second = lax.ppermute(far, "slab", second)
    out = call(
        weight_final_kernel, "weight_final", [far, got_first, got_second], [(3, CH // 2, CH)], 4
    )[0]
    return jnp.transpose(out, (1, 0, 2))


def text_final_kernel(full, twin, key, value):
    _, _, _, _, core = place()
    key[...] = jnp.where(core == 0, full[...], twin[...])
    value[...] = jnp.where(core == 0, twin[...], full[...])


def text_step(part, bit):
    got = lax.ppermute(part, "slab", [(s, s ^ bit) for s in range(16)])
    return call(sum_kernel, "text_pair", [part, got], [part.shape], 4)[0]


def text_final(part):
    both = [part, slab_move(part, 0, 0, 1)]
    return jnp.stack(call(text_final_kernel, "text_final", both, [part.shape] * 2, 4), axis=2)


def body(hidden, w_qkv, text_keys, text_values, text_len, advantage, out_grad, tile_lists):
    w = jnp.transpose(w_qkv, (1, 0, 2)).reshape(3, 2, 4, CH, CH)
    scalars = (tile_lists, text_len, advantage)
    w, q, *kvs, mine, other = project(hidden, w)
    halos = [(slab_step(kvs[0], 1), slab_step(kvs[0], -1))]
    halos, other, late = lax.optimization_barrier((halos, other, kvs[1]))
    theirs = slab_move(other, 0, 0, 1)
    halos.append((slab_step(late, 1), slab_step(late, -1)))
    ends, keeps, swap = ([], [], None)
    for s in range(SAMPLES):
        if s == 1:
            q, _, theirs = lax.optimization_barrier((q, swap, theirs))
        swap, dprev, down, dnext, keep = attention(
            s, scalars, q, halos[s][0], kvs[s], halos[s][1], text_keys, text_values, out_grad, swap
        )
        keeps.append(keep)
        ends.append((down, dnext, dprev))
    sums = [(ends[0][0], slab_step(ends[0][1], 1), slab_step(ends[0][2], -1))]
    down, dnext, dprev = ends[1]
    sums, swap, dnext, dprev = lax.optimization_barrier((sums, swap, dnext, dprev))
    sums.append((down, slab_step(dnext, 1), slab_step(dprev, -1)))
    swap_twin = slab_move(swap, 0, 0, 1)
    *query, text = query_weight_parts(mine, theirs, swap, swap_twin, *keeps)
    grad, _ = lax.optimization_barrier((total(*sums[0]), text))
    first, *parts = hidden_parts(0, swap, grad, w, [])
    first = head_move(first, 0, 3)
    text = text_step(text, 4)
    sums[1], _, text = lax.optimization_barrier((sums[1], parts, text))
    grads = call(join_kernel, "join", [grad, *sums[1]], [(SAMPLES, TILE, 2 * CH)], 4)[0]
    twin = slab_move(grads, 0, 0, 1)
    last_flip, last_same, *parts = hidden_parts(1, swap, grads, w, parts)
    last = (head_move(last_flip, 0, 1), head_move(last_same, 0, 3))
    text = text_step(text, 8)
    twin, _, text = lax.optimization_barrier((twin, last_flip, text))
    rest = weight_parts([mine, theirs, grads, twin], query)
    hidden_grad, text = hidden_reduce(first, *last, parts, text)
    text = text_step(text, 2)
    ring, text = weight_ring(text, *rest)
    text_grad = text_final(text)
    weight_grad = weight_home(ring)
    return (hidden_grad, weight_grad, text_grad)


def solution(mesh):
    in_specs = (
        P("slab", "head"),
        P(None, None, "head"),
        P(None, None, "head"),
        P(None, None, "head"),
        P(),
        P(),
        P("slab", "head"),
        P("slab", None),
    )
    out_specs = (P("slab", "head"), P("slab", None, "head"), P(None, None, None, "head"))
    return jax.shard_map(body, mesh=mesh, in_specs=in_specs, out_specs=out_specs, check_vma=False)
```

```python
import functools
import math

import jax
import jax.numpy as jnp
from jax import lax
from jax.experimental import pallas as pl
from jax.experimental.pallas import tpu as pltpu
from jax.sharding import PartitionSpec as P

DH = 128
TILE = 384
SAMPLES = 2
HEADS_DEV = 3
CH = 384
TEXT = 256
BF = jnp.bfloat16
F32 = jnp.float32
SCALE = 1.0 / math.sqrt(DH)
EXP_SCALE = SCALE * math.log2(math.e)
MIB = 1024 * 1024
TIMES = {'load': 9.0, 'project': 14.4, 'project_late': 4.8, 'attention': 24.6, 'join': 2.1, 'hidden_parts': 11.7, 'query_weight_parts': 8.25, 'weight_parts': 11.4, 'hidden_far': 1.35, 'hidden_near': 3.45, 'hidden_sum': 3.3, 'weight_far': 1.95, 'weight_halves': 1.8, 'weight_final': 2.7, 'text_pair': 1.5, 'text_final': 1.5}


def cost(name):
    return pl.CostEstimate(flops=int(TIMES[name] * 1.15e9), bytes_accessed=10**4, transcendentals=0)

VMEM = pl.BlockSpec(memory_space=pltpu.VMEM)
SMEM = pl.BlockSpec(memory_space=pltpu.SMEM)


def dot(a, b, ca, cb):
    return lax.dot_general(a, b, (((ca,), (cb,)), ((), ())), preferred_element_type=F32)


def head_move(x, dx, dy):
    pairs = [(h, ((h // 4) ^ dx) * 4 + (h + dy) % 4) for h in range(8)]
    return lax.ppermute(x, "head", pairs)


def slab_move(x, dz, dx, dc):
    pairs = [
        (s, ((s // 4 + dz) % 4) * 4 + ((s // 2 % 2) ^ dx) * 2 + ((s % 2) ^ dc)) for s in range(16)
    ]
    return lax.ppermute(x, "slab", pairs)


def slab_step(x, distance):
    pairs = [(i, (i + distance) % 16) for i in range(16)]
    return lax.ppermute(x, "slab", pairs)


def place():
    slab, head = (lax.axis_index("slab"), lax.axis_index("head"))
    return (head >> 2, head & 3, slab >> 2, (slab >> 1) & 1, slab & 1)


def call(kernel, name, arrays, shapes, limit, scratch=(), **options):
    return pl.pallas_call(
        kernel,
        in_specs=[VMEM] * len(arrays),
        out_specs=[VMEM] * len(shapes),
        out_shape=[jax.ShapeDtypeStruct(shape, BF) for shape in shapes],
        scratch_shapes=list(scratch),
        compiler_params=pltpu.CompilerParams(vmem_limit_bytes=limit * MIB),
        cost_estimate=cost(name),
        name=name,
        **options,
    )(*arrays)


def total(*refs):
    value = refs[0].astype(F32)
    for ref in refs[1:]:
        value = value + ref.astype(F32)
    return value.astype(BF)


ROWS = SAMPLES * TILE
FIRST = ((0, 0, 1), (3, 2, None), (1, 3, None))
SECOND = ((3, None, 0), (1, None, 1), (2, 2, None))


def load_kernel(w, out, sem):
    copy = pltpu.make_async_copy(w, out, sem)
    copy.start()
    copy.wait()


def load(w):
    return pl.pallas_call(
        load_kernel,
        in_specs=[pl.BlockSpec(memory_space=pl.ANY)],
        out_specs=VMEM,
        out_shape=jax.ShapeDtypeStruct(w.shape, BF),
        scratch_shapes=[pltpu.SemaphoreType.DMA],
        compiler_params=pltpu.CompilerParams(vmem_limit_bytes=MIB),
        cost_estimate=cost("load"),
        name="load",
    )(w)


def place_chunk(ref, a, yj, core, mine, other):
    z = (a * 4 + yj) >> 1
    own = ((yj ^ core) & 1) == 0

    @pl.when(own)
    def _():
        mine[z] = ref[...]

    @pl.when(jnp.logical_not(own))
    def _():
        other[z] = ref[...]


def project_kernel(steps, count, *refs):
    chunks, w, rest = (refs[:count], refs[count], refs[count + 1 :])
    acc, mine, other = rest[-3:]
    start = rest[0] if len(rest) > 3 else None
    a, y, _, _, core = place()
    for n, (d, r0, r1) in enumerate(steps):
        yj = (y + d) & 3
        pair = [(r, chunks[i]) for r, i in ((a, r0), (1 - a, r1)) if i is not None]
        for r, ref in pair:
            place_chunk(ref, r, yj, core, mine, other)
        x = jnp.concatenate([ref[...] for _, ref in pair], axis=1)
        for c in range(3):
            wc = jnp.concatenate([w[c, r, yj] for r, _ in pair], axis=0)
            part = dot(x, wc, 1, 0)
            if n > 0:
                acc[c] += part
            elif start is None:
                acc[c] = part
            else:
                acc[c] = start[c] + part


def project_step(steps, chunks, w, before):
    count = len(chunks)
    return pl.pallas_call(
        functools.partial(project_kernel, steps, count),
        in_specs=[VMEM] * (count + 1 + len(before)),
        out_specs=[VMEM] * 3,
        out_shape=[
            jax.ShapeDtypeStruct((3, ROWS, CH), F32),
            jax.ShapeDtypeStruct((4, ROWS, CH), BF),
            jax.ShapeDtypeStruct((4, ROWS, CH), BF),
        ],
        input_output_aliases={count + 1 + n: n for n in range(len(before))},
        compiler_params=pltpu.CompilerParams(vmem_limit_bytes=6 * MIB),
        cost_estimate=cost("project"),
        name="project",
    )(*chunks, w, *before)


def project_late_kernel(first, second, w, acc, mine_in, other_in, q_out, *refs):
    kv_outs, (mine, other, last) = (refs[:SAMPLES], refs[SAMPLES:])
    a, y, _, _, core = place()
    yj = (y + 2) & 3
    last[:TILE] = first[...]
    last[TILE:] = second[...]
    place_chunk(last, 1 - a, yj, core, mine, other)
    for c in (1, 2, 0):
        part = (acc[c] + dot(last[...], w[c, 1 - a, yj], 1, 0)).astype(BF)
        if c == 0:
            q_out[...] = part
            continue
        for s, kv_out in enumerate(kv_outs):
            for h in range(HEADS_DEV):
                at = (2 * h + c - 1) * DH
                kv_out[:, at : at + DH] = part[s * TILE : (s + 1) * TILE, h * DH : (h + 1) * DH]


def project(hidden, w):
    flip = head_move(hidden, 1, 0)
    below = head_move(hidden, 0, 1)
    above = head_move(hidden, 0, 3)
    flip, below, above, w = lax.optimization_barrier((flip, below, above, load(w)))
    flip_below = head_move(below, 1, 0)
    flip_above = head_move(flip, 0, 3)
    far = head_move(below, 0, 1)
    sums = project_step(FIRST, [hidden, flip, below, above], w, [])
    late = [flip_below, flip_above, far]
    late, sums = lax.optimization_barrier((late, sums))
    last = [head_move(late[0][:TILE], 0, 1), head_move(late[1][TILE:], 0, 3)]
    acc, mine, other = project_step(SECOND, late, w, sums)
    shapes = [(ROWS, CH), (TILE, 2 * CH), (TILE, 2 * CH), (4, ROWS, CH), (4, ROWS, CH)]
    outs = call(
        project_late_kernel,
        "project_late",
        [*last, w, acc, mine, other],
        shapes,
        6,
        [pltpu.VMEM((ROWS, CH), BF)],
        input_output_aliases={4: 3, 5: 4},
    )
    return (w, *outs)


def attention_kernel(
    sample,
    lists,
    lengths,
    adv,
    q_ref,
    prev,
    own,
    nxt,
    tk_ref,
    tv_ref,
    og_ref,
    *refs,
):
    swap, dprev, down, dnext, keep = refs[-5:]
    slab = lax.axis_index("slab")
    tile = slab * SAMPLES + sample
    before, after = (False, False)
    for n in range(lists.shape[1]):
        before = before | (lists[sample, n] == tile - SAMPLES)
        after = after | (lists[sample, n] == tile + SAMPLES)
    before = before & (slab > 0)
    q = q_ref[...]
    cot = (adv[sample] * og_ref[...].astype(F32)).astype(BF)
    rows = lax.broadcasted_iota(jnp.int32, (TEXT, TILE), 0)
    live = rows < lengths[sample]
    keys = [prev[:, :DH], own[:, :DH], nxt[:, :DH], tk_ref[0]]
    vals = [prev[:, DH:], own[:, DH:], nxt[:, DH:], tv_ref[0]]
    scores = [dot(k, q, 1, 1) for k in keys]
    scores[0] = jnp.where(before, scores[0], -jnp.inf)
    scores[2] = jnp.where(after, scores[2], -jnp.inf)
    scores[3] = jnp.where(live, scores[3], -jnp.inf)
    top = jnp.max(scores[1], axis=0, keepdims=True)
    for n in (0, 2, 3):
        top = jnp.maximum(top, jnp.max(scores[n], axis=0, keepdims=True))
    powers = [jnp.exp2((s - top) * EXP_SCALE) for s in scores]
    total = sum(jnp.sum(p, axis=0, keepdims=True) for p in powers)
    inverse = 1.0 / total
    probs = [p * inverse for p in powers]
    probs_b = [p.astype(BF) for p in probs]
    dprobs = [dot(v, cot, 1, 1) for v in vals]
    delta = sum(
        jnp.sum(p.astype(F32) * d, axis=0, keepdims=True) for p, d in zip(probs_b, dprobs)
    )
    dscores = [(p * (d - delta) * SCALE).astype(BF) for p, d in zip(probs, dprobs)]
    grad = dot(keys[0], dscores[0], 0, 0)
    for n in (1, 2, 3):
        grad += dot(keys[n], dscores[n], 0, 0)
    swap[0, :TILE] = grad.T.astype(BF)
    for n, out in ((0, dprev), (1, down), (2, dnext)):
        out[:, :DH] = dot(dscores[n], q, 1, 0).astype(out.dtype)
        out[:, DH:] = dot(probs_b[n], cot, 1, 0).astype(out.dtype)
    text_key = dot(dscores[3], q, 1, 0).astype(BF)
    text_value = dot(probs_b[3], cot, 1, 0).astype(BF)
    first = (slab & 1) == 0
    keep[...] = jnp.where(first, text_key, text_value)
    swap[0, TILE:] = jnp.where(first, text_value, text_key)


def attention(sample, scalars, q, prev, own, nxt, text_k, text_v, out_grad, swap):
    kv = pl.BlockSpec((TILE, 2 * DH), lambda h: (0, h))
    tile = pl.BlockSpec((TILE, DH), lambda h: (sample, h))
    text = pl.BlockSpec((1, TEXT, DH), lambda h: (sample, 0, h))
    arrays = [*scalars, q, prev, own, nxt, text_k, text_v, out_grad]
    in_specs = [SMEM, SMEM, SMEM, tile, kv, kv, kv, text, text, tile]
    aliases = {}
    if swap is not None:
        aliases = {len(arrays): 0}
        arrays.append(swap)
        in_specs.append(pl.BlockSpec(memory_space=pl.ANY))
    return pl.pallas_call(
        functools.partial(attention_kernel, sample),
        grid=(HEADS_DEV,),
        in_specs=in_specs,
        out_specs=[
            pl.BlockSpec((1, TILE + TEXT, DH), lambda h: (sample, 0, h)),
            kv,
            kv,
            kv,
            pl.BlockSpec((TEXT, DH), lambda h: (0, h)),
        ],
        out_shape=[
            jax.ShapeDtypeStruct((SAMPLES, TILE + TEXT, CH), BF),
            jax.ShapeDtypeStruct((TILE, 2 * CH), BF),
            jax.ShapeDtypeStruct((TILE, 2 * CH), F32),
            jax.ShapeDtypeStruct((TILE, 2 * CH), BF),
            jax.ShapeDtypeStruct((TEXT, CH), BF),
        ],
        input_output_aliases=aliases,
        compiler_params=pltpu.CompilerParams(vmem_limit_bytes=12 * MIB),
        cost_estimate=cost("attention"),
        name="attention",
    )(*arrays)


def join_kernel(before, down, low, high, out):
    out[0] = before[...]
    out[1] = total(down[...], low[...], high[...])


REDUCE = ((2, "far", "flip_far"), (3, "below", "flip_below"), (1, "above", "flip_above"), (0, "own", "flip"))
PARTS = ("below", "flip_below", "above", "flip_above", "own", "flip")


def hidden_kernel(sample, swap, grads, w, *refs):
    outs = dict(zip(PARTS, refs[-len(PARTS) :], strict=True))
    ends = refs[-len(PARTS) - 1 - sample : -len(PARTS)]
    kv = grads.at[sample] if len(grads.shape) == 3 else grads
    rows = slice(sample * TILE, (sample + 1) * TILE)
    a, y, _, _, _ = place()
    keys = [kv[:, 2 * h * DH : (2 * h + 1) * DH] for h in range(HEADS_DEV)]
    vals = [kv[:, (2 * h + 1) * DH : (2 * h + 2) * DH] for h in range(HEADS_DEV)]
    g = [swap[sample, :TILE], jnp.concatenate(keys, axis=1), jnp.concatenate(vals, axis=1)]
    for d, same, flip in REDUCE:
        yj = (y + d) & 3
        part = None
        for c in range(3):
            wc = jnp.concatenate([w[c, a, yj], w[c, 1 - a, yj]], axis=0)
            term = dot(g[c], wc, 1, 1)
            part = term if part is None else part + term
        part = part.astype(BF)
        if d != 2:
            outs[same][rows] = part[:, :CH]
            outs[flip][rows] = part[:, CH:]
        elif sample == 0:
            ends[0][:TILE] = part[:, CH:]
            ends[0][TILE:] = part[:, :CH]
        else:
            ends[0][...] = part[:, CH:]
            ends[1][...] = part[:, :CH]


def hidden_parts(sample, swap, grads, w, before):
    ends = [(ROWS, CH)] if sample == 0 else [(TILE, CH)] * 2
    arrays = [swap, grads, w, *before]
    return call(
        functools.partial(hidden_kernel, sample),
        "hidden_parts",
        arrays,
        ends + [(ROWS, CH)] * len(PARTS),
        4,
        input_output_aliases={3 + n: len(ends) + n for n in range(len(before))},
    )


def far_kernel(below, above, got_below, got_above, below_out, above_out):
    below_out[:TILE] = total(below[:TILE], got_below[:TILE])
    below_out[TILE:] = below[TILE:]
    above_out[:TILE] = above[:TILE]
    above_out[TILE:] = total(above[TILE:], got_above[...])


def near_kernel(below, flip, flip_below, flip_above, first, second, below_out, flip_out):
    below_out[:TILE] = total(below[:TILE], flip_below[:TILE], first[TILE:])
    below_out[TILE:] = total(below[TILE:], flip_below[TILE:], second[...])
    flip_out[...] = total(flip[...], flip_above[...])


def sum_kernel(*refs):
    refs[-1][...] = total(*[r[...] for r in refs[:-1]])


def hidden_reduce(first, got_flip, got_same, parts, text):
    part = dict(zip(PARTS, parts, strict=True))
    both = [(ROWS, CH)] * 2
    sides = [part["flip_below"], part["flip_above"], first, got_flip]
    flip_below, flip_above = call(
        far_kernel, "hidden_far", sides, both, 4, input_output_aliases={0: 0, 1: 1}
    )
    got = [head_move(flip_below, 1, 0), head_move(flip_above, 0, 1)]
    sides = [part["below"], part["flip"], *got, first, got_same]
    below, flip = call(
        near_kernel, "hidden_near", sides, both, 4, input_output_aliases={0: 0, 1: 1}
    )
    got = [head_move(below, 0, 3), head_move(part["above"], 0, 1), head_move(flip, 1, 0)]
    return (call(sum_kernel, "hidden_sum", [part["own"], *got], both[:1], 4)[0], text)


RING = [(CH // 2, 3 * CH)] * 2 + [(CH, 3 * CH)] * 3


def ring_store(outs, n, cols, part):
    if n == 0:
        outs[0][:, cols] = part[: CH // 2]
        outs[1][:, cols] = part[CH // 2 :]
    else:
        outs[n + 1][:, cols] = part


def query_weight_kernel(x_own, x_twin, own, twin, keep0, keep1, *outs):
    _, _, z, _, _ = place()
    g = jnp.concatenate([r[s, :TILE] for r in (own, twin) for s in range(SAMPLES)], axis=0)
    for s, keep in enumerate((keep0, keep1)):
        outs[5][s] = total(keep[...], twin[s, TILE:])
    for n, d in enumerate((2, 1, 3, 0)):
        j = (z + d) & 3
        x = jnp.concatenate([x_own[j], x_twin[j]], axis=0)
        ring_store(outs, n, slice(0, CH), dot(x, g, 0, 0).astype(BF))


def query_weight_parts(*arrays):
    shapes = [*RING, (SAMPLES, TEXT, CH)]
    return call(query_weight_kernel, "query_weight_parts", arrays, shapes, 4)


def weight_kernel(x_own, x_twin, own, twin, *refs):
    outs = refs[len(RING) :]
    _, _, z, _, _ = place()
    g = jnp.concatenate([r[s] for r in (own, twin) for s in range(SAMPLES)], axis=0)
    for n, d in enumerate((2, 1, 3, 0)):
        j = (z + d) & 3
        x = jnp.concatenate([x_own[j], x_twin[j]], axis=0)
        part = dot(x, g, 0, 0).astype(BF)
        for h in range(HEADS_DEV):
            for k in range(2):
                at, to = ((2 * h + k) * DH, (k + 1) * CH + h * DH)
                ring_store(outs, n, slice(to, to + DH), part[:, at : at + DH])


def weight_parts(arrays, before):
    aliases = {len(arrays) + n: n for n in range(len(RING))}
    arrays = [*arrays, *before]
    return call(weight_kernel, "weight_parts", arrays, RING, 6, input_output_aliases=aliases)


def weight_far_kernel(up, down, got_up, got_down, up_out, down_out):
    half = CH // 2
    up_out[:half] = total(up[:half], got_up[...])
    up_out[half:] = up[half:]
    down_out[:half] = down[:half]
    down_out[half:] = total(down[half:], got_down[...])


def weight_ring(text, far_up, far_down, up, down, own):
    got = [slab_move(far_up, 1, 0, 0), slab_move(far_down, 3, 0, 0)]
    got, text = lax.optimization_barrier((got, text))
    both = RING[3:]
    up, down = call(
        weight_far_kernel, "weight_far", [up, down, *got], both, 4, input_output_aliases={0: 0, 1: 1}
    )
    return ([own, slab_move(up, 1, 0, 0), slab_move(down, 3, 0, 0)], text)


def weight_halves_kernel(own, up, down, near, far):
    _, _, _, x, core = place()
    home = x == core
    for half in range(2):
        rows = slice(half * CH // 2, (half + 1) * CH // 2)
        part = total(own[rows], up[rows], down[rows])
        is_far = (core == half) == home

        @pl.when(is_far)
        def _():
            far[...] = part

        @pl.when(jnp.logical_not(is_far))
        def _():
            near[...] = part


def weight_final_kernel(far, got_first, got_second, out):
    _, _, _, x, core = place()
    for c in range(3):
        cols = slice(c * CH, (c + 1) * CH)
        kept = jnp.where(x == core, far[:, cols], got_second[:, cols])
        out[c] = total(kept, got_first[:, cols])


def weight_home(parts):
    half = (CH // 2, 3 * CH)
    near, far = call(weight_halves_kernel, "weight_halves", parts, [half, half], 6)
    first, second = ([], [])
    for s in range(16):
        z, x, c = (s // 4, s // 2 % 2, s % 2)
        if x == c:
            first.append((s, z * 4 + x * 2 + 1 - c))
        else:
            first.append((s, z * 4 + (1 - x) * 2 + c))
            second.append((s, z * 4 + (1 - x) * 2 + 1 - c))
    got_first = lax.ppermute(near, "slab", first)
    got_second = lax.ppermute(far, "slab", second)
    out = call(
        weight_final_kernel, "weight_final", [far, got_first, got_second], [(3, CH // 2, CH)], 4
    )[0]
    return jnp.transpose(out, (1, 0, 2))


def text_final_kernel(full, twin, key, value):
    _, _, _, _, core = place()
    key[...] = jnp.where(core == 0, full[...], twin[...])
    value[...] = jnp.where(core == 0, twin[...], full[...])


def text_step(part, bit):
    got = lax.ppermute(part, "slab", [(s, s ^ bit) for s in range(16)])
    return call(sum_kernel, "text_pair", [part, got], [part.shape], 4)[0]


def text_final(part):
    both = [part, slab_move(part, 0, 0, 1)]
    return jnp.stack(call(text_final_kernel, "text_final", both, [part.shape] * 2, 4), axis=2)


def body(hidden, w_qkv, text_keys, text_values, text_len, advantage, out_grad, tile_lists):
    w = jnp.transpose(w_qkv, (1, 0, 2)).reshape(3, 2, 4, CH, CH)
    scalars = (tile_lists, text_len, advantage)
    w, q, *kvs, mine, other = project(hidden, w)
    halos = [(slab_step(kvs[0], 1), slab_step(kvs[0], -1))]
    late = kvs[1]
    halos, other = lax.optimization_barrier((halos, other))
    theirs = slab_move(other, 0, 0, 1)
    halos.append((slab_step(late, 1), slab_step(late, -1)))
    ends, keeps, swap = ([], [], None)
    for s in range(SAMPLES):
        if s == 1:
            q, _, theirs = lax.optimization_barrier((q, swap, theirs))
        swap, dprev, down, dnext, keep = attention(
            s, scalars, q, halos[s][0], kvs[s], halos[s][1], text_keys, text_values, out_grad, swap
        )
        keeps.append(keep)
        ends.append((down, dnext, dprev))
    sums = [(ends[0][0], slab_step(ends[0][1], 1), slab_step(ends[0][2], -1))]
    down, dnext, dprev = ends[1]
    sums, swap, dnext, dprev = lax.optimization_barrier((sums, swap, dnext, dprev))
    sums.append((down, slab_step(dnext, 1), slab_step(dprev, -1)))
    swap_twin = slab_move(swap, 0, 0, 1)
    *query, text = query_weight_parts(mine, theirs, swap, swap_twin, *keeps)
    grad, _ = lax.optimization_barrier((total(*sums[0]), text))
    first, *parts = hidden_parts(0, swap, grad, w, [])
    first = head_move(first, 0, 3)
    text = text_step(text, 4)
    sums[1], _, text = lax.optimization_barrier((sums[1], parts, text))
    grads = call(join_kernel, "join", [grad, *sums[1]], [(SAMPLES, TILE, 2 * CH)], 4)[0]
    twin = slab_move(grads, 0, 0, 1)
    last_flip, last_same, *parts = hidden_parts(1, swap, grads, w, parts)
    last = (head_move(last_flip, 0, 1), head_move(last_same, 0, 3))
    text = text_step(text, 8)
    twin, _, text = lax.optimization_barrier((twin, last_flip, text))
    rest = weight_parts([mine, theirs, grads, twin], query)
    hidden_grad, text = hidden_reduce(first, *last, parts, text)
    text = text_step(text, 2)
    ring, text = weight_ring(text, *rest)
    text_grad = text_final(text)
    weight_grad = weight_home(ring)
    return (hidden_grad, weight_grad, text_grad)


def solution(mesh):
    in_specs = (
        P("slab", "head"),
        P(None, None, "head"),
        P(None, None, "head"),
        P(None, None, "head"),
        P(),
        P(),
        P("slab", "head"),
        P("slab", None),
    )
    out_specs = (P("slab", "head"), P("slab", None, "head"), P(None, None, None, "head"))
    return jax.shard_map(body, mesh=mesh, in_specs=in_specs, out_specs=out_specs, check_vma=False)
```

```python
import functools
import math

import jax
import jax.numpy as jnp
from jax import lax
from jax.experimental import pallas as pl
from jax.experimental.pallas import tpu as pltpu
from jax.sharding import PartitionSpec as P

DH = 128
TILE = 384
SAMPLES = 2
HEADS_DEV = 3
CH = 384
TEXT = 256
BF = jnp.bfloat16
F32 = jnp.float32
SCALE = 1.0 / math.sqrt(DH)
EXP_SCALE = SCALE * math.log2(math.e)
MIB = 1024 * 1024
TIMES = {'load': 9.0, 'project': 14.4, 'project_late': 4.8, 'attention': 24.6, 'join': 2.1, 'hidden_parts': 11.7, 'query_weight_parts': 8.25, 'weight_parts': 11.4, 'hidden_far': 1.35, 'hidden_near': 3.45, 'hidden_sum': 3.3, 'weight_far': 1.95, 'weight_halves': 1.8, 'weight_final': 2.7, 'text_pair': 1.5, 'text_final': 1.5}


def cost(name):
    return pl.CostEstimate(flops=int(TIMES[name] * 1.15e9), bytes_accessed=10**4, transcendentals=0)

VMEM = pl.BlockSpec(memory_space=pltpu.VMEM)
SMEM = pl.BlockSpec(memory_space=pltpu.SMEM)


def dot(a, b, ca, cb):
    return lax.dot_general(a, b, (((ca,), (cb,)), ((), ())), preferred_element_type=F32)


def head_move(x, dx, dy):
    pairs = [(h, ((h // 4) ^ dx) * 4 + (h + dy) % 4) for h in range(8)]
    return lax.ppermute(x, "head", pairs)


def slab_move(x, dz, dx, dc):
    pairs = [
        (s, ((s // 4 + dz) % 4) * 4 + ((s // 2 % 2) ^ dx) * 2 + ((s % 2) ^ dc)) for s in range(16)
    ]
    return lax.ppermute(x, "slab", pairs)


def slab_step(x, distance):
    pairs = [(i, (i + distance) % 16) for i in range(16)]
    return lax.ppermute(x, "slab", pairs)


def place():
    slab, head = (lax.axis_index("slab"), lax.axis_index("head"))
    return (head >> 2, head & 3, slab >> 2, (slab >> 1) & 1, slab & 1)


def call(kernel, name, arrays, shapes, limit, scratch=(), **options):
    return pl.pallas_call(
        kernel,
        in_specs=[VMEM] * len(arrays),
        out_specs=[VMEM] * len(shapes),
        out_shape=[jax.ShapeDtypeStruct(shape, BF) for shape in shapes],
        scratch_shapes=list(scratch),
        compiler_params=pltpu.CompilerParams(vmem_limit_bytes=limit * MIB),
        cost_estimate=cost(name),
        name=name,
        **options,
    )(*arrays)


def total(*refs):
    value = refs[0].astype(F32)
    for ref in refs[1:]:
        value = value + ref.astype(F32)
    return value.astype(BF)


ROWS = SAMPLES * TILE
FIRST = ((0, 0, 1), (3, 2, None), (1, 3, None))
SECOND = ((3, None, 0), (1, None, 1), (2, 2, None))


def load_kernel(w, out, sem):
    copy = pltpu.make_async_copy(w, out, sem)
    copy.start()
    copy.wait()


def load(w):
    return pl.pallas_call(
        load_kernel,
        in_specs=[pl.BlockSpec(memory_space=pl.ANY)],
        out_specs=VMEM,
        out_shape=jax.ShapeDtypeStruct(w.shape, BF),
        scratch_shapes=[pltpu.SemaphoreType.DMA],
        compiler_params=pltpu.CompilerParams(vmem_limit_bytes=MIB),
        cost_estimate=cost("load"),
        name="load",
    )(w)


def place_chunk(ref, a, yj, core, mine, other):
    z = (a * 4 + yj) >> 1
    own = ((yj ^ core) & 1) == 0

    @pl.when(own)
    def _():
        mine[z] = ref[...]

    @pl.when(jnp.logical_not(own))
    def _():
        other[z] = ref[...]


def project_kernel(steps, count, *refs):
    chunks, w, rest = (refs[:count], refs[count], refs[count + 1 :])
    acc, mine, other = rest[-3:]
    start = rest[0] if len(rest) > 3 else None
    a, y, _, _, core = place()
    for n, (d, r0, r1) in enumerate(steps):
        yj = (y + d) & 3
        pair = [(r, chunks[i]) for r, i in ((a, r0), (1 - a, r1)) if i is not None]
        for r, ref in pair:
            place_chunk(ref, r, yj, core, mine, other)
        x = jnp.concatenate([ref[...] for _, ref in pair], axis=1)
        for c in range(3):
            wc = jnp.concatenate([w[c, r, yj] for r, _ in pair], axis=0)
            part = dot(x, wc, 1, 0)
            if n > 0:
                acc[c] += part
            elif start is None:
                acc[c] = part
            else:
                acc[c] = start[c] + part


def project_step(steps, chunks, w, before):
    count = len(chunks)
    return pl.pallas_call(
        functools.partial(project_kernel, steps, count),
        in_specs=[VMEM] * (count + 1 + len(before)),
        out_specs=[VMEM] * 3,
        out_shape=[
            jax.ShapeDtypeStruct((3, ROWS, CH), F32),
            jax.ShapeDtypeStruct((4, ROWS, CH), BF),
            jax.ShapeDtypeStruct((4, ROWS, CH), BF),
        ],
        input_output_aliases={count + 1 + n: n for n in range(len(before))},
        compiler_params=pltpu.CompilerParams(vmem_limit_bytes=6 * MIB),
        cost_estimate=cost("project"),
        name="project",
    )(*chunks, w, *before)


def project_late_kernel(first, second, w, acc, mine_in, other_in, q_out, *refs):
    kv_outs, (mine, other, last) = (refs[:SAMPLES], refs[SAMPLES:])
    a, y, _, _, core = place()
    yj = (y + 2) & 3
    last[:TILE] = first[...]
    last[TILE:] = second[...]
    place_chunk(last, 1 - a, yj, core, mine, other)
    for c in (1, 2, 0):
        part = (acc[c] + dot(last[...], w[c, 1 - a, yj], 1, 0)).astype(BF)
        if c == 0:
            q_out[...] = part
            continue
        for s, kv_out in enumerate(kv_outs):
            for h in range(HEADS_DEV):
                at = (2 * h + c - 1) * DH
                kv_out[:, at : at + DH] = part[s * TILE : (s + 1) * TILE, h * DH : (h + 1) * DH]


def project(hidden, w):
    flip = head_move(hidden, 1, 0)
    below = head_move(hidden, 0, 1)
    above = head_move(hidden, 0, 3)
    below, above, w = lax.optimization_barrier((below, above, load(w)))
    flip_below = head_move(below, 1, 0)
    flip_above = head_move(flip, 0, 3)
    far = head_move(below, 0, 1)
    sums = project_step(FIRST, [hidden, flip, below, above], w, [])
    late = [flip_below, flip_above, far]
    late, sums = lax.optimization_barrier((late, sums))
    last = [head_move(late[0][:TILE], 0, 1), head_move(late[1][TILE:], 0, 3)]
    acc, mine, other = project_step(SECOND, late, w, sums)
    shapes = [(ROWS, CH), (TILE, 2 * CH), (TILE, 2 * CH), (4, ROWS, CH), (4, ROWS, CH)]
    outs = call(
        project_late_kernel,
        "project_late",
        [*last, w, acc, mine, other],
        shapes,
        6,
        [pltpu.VMEM((ROWS, CH), BF)],
        input_output_aliases={4: 3, 5: 4},
    )
    return (w, *outs)


def attention_kernel(
    sample,
    lists,
    lengths,
    adv,
    q_ref,
    prev,
    own,
    nxt,
    tk_ref,
    tv_ref,
    og_ref,
    *refs,
):
    swap, dprev, down, dnext, keep = refs[-5:]
    slab = lax.axis_index("slab")
    tile = slab * SAMPLES + sample
    before, after = (False, False)
    for n in range(lists.shape[1]):
        before = before | (lists[sample, n] == tile - SAMPLES)
        after = after | (lists[sample, n] == tile + SAMPLES)
    before = before & (slab > 0)
    q = q_ref[...]
    cot = (adv[sample] * og_ref[...].astype(F32)).astype(BF)
    rows = lax.broadcasted_iota(jnp.int32, (TEXT, TILE), 0)
    live = rows < lengths[sample]
    keys = [prev[:, :DH], own[:, :DH], nxt[:, :DH], tk_ref[0]]
    vals = [prev[:, DH:], own[:, DH:], nxt[:, DH:], tv_ref[0]]
    scores = [dot(k, q, 1, 1) for k in keys]
    scores[0] = jnp.where(before, scores[0], -jnp.inf)
    scores[2] = jnp.where(after, scores[2], -jnp.inf)
    scores[3] = jnp.where(live, scores[3], -jnp.inf)
    top = jnp.max(scores[1], axis=0, keepdims=True)
    for n in (0, 2, 3):
        top = jnp.maximum(top, jnp.max(scores[n], axis=0, keepdims=True))
    powers = [jnp.exp2((s - top) * EXP_SCALE) for s in scores]
    total = sum(jnp.sum(p, axis=0, keepdims=True) for p in powers)
    inverse = 1.0 / total
    probs = [p * inverse for p in powers]
    probs_b = [p.astype(BF) for p in probs]
    dprobs = [dot(v, cot, 1, 1) for v in vals]
    delta = sum(
        jnp.sum(p.astype(F32) * d, axis=0, keepdims=True) for p, d in zip(probs_b, dprobs)
    )
    dscores = [(p * (d - delta) * SCALE).astype(BF) for p, d in zip(probs, dprobs)]
    grad = dot(keys[0], dscores[0], 0, 0)
    for n in (1, 2, 3):
        grad += dot(keys[n], dscores[n], 0, 0)
    swap[0, :TILE] = grad.T.astype(BF)
    for n, out in ((0, dprev), (1, down), (2, dnext)):
        out[:, :DH] = dot(dscores[n], q, 1, 0).astype(out.dtype)
        out[:, DH:] = dot(probs_b[n], cot, 1, 0).astype(out.dtype)
    text_key = dot(dscores[3], q, 1, 0).astype(BF)
    text_value = dot(probs_b[3], cot, 1, 0).astype(BF)
    first = (slab & 1) == 0
    keep[...] = jnp.where(first, text_key, text_value)
    swap[0, TILE:] = jnp.where(first, text_value, text_key)


def attention(sample, scalars, q, prev, own, nxt, text_k, text_v, out_grad, swap):
    kv = pl.BlockSpec((TILE, 2 * DH), lambda h: (0, h))
    tile = pl.BlockSpec((TILE, DH), lambda h: (sample, h))
    text = pl.BlockSpec((1, TEXT, DH), lambda h: (sample, 0, h))
    arrays = [*scalars, q, prev, own, nxt, text_k, text_v, out_grad]
    in_specs = [SMEM, SMEM, SMEM, tile, kv, kv, kv, text, text, tile]
    aliases = {}
    if swap is not None:
        aliases = {len(arrays): 0}
        arrays.append(swap)
        in_specs.append(pl.BlockSpec(memory_space=pl.ANY))
    return pl.pallas_call(
        functools.partial(attention_kernel, sample),
        grid=(HEADS_DEV,),
        in_specs=in_specs,
        out_specs=[
            pl.BlockSpec((1, TILE + TEXT, DH), lambda h: (sample, 0, h)),
            kv,
            kv,
            kv,
            pl.BlockSpec((TEXT, DH), lambda h: (0, h)),
        ],
        out_shape=[
            jax.ShapeDtypeStruct((SAMPLES, TILE + TEXT, CH), BF),
            jax.ShapeDtypeStruct((TILE, 2 * CH), BF),
            jax.ShapeDtypeStruct((TILE, 2 * CH), F32),
            jax.ShapeDtypeStruct((TILE, 2 * CH), BF),
            jax.ShapeDtypeStruct((TEXT, CH), BF),
        ],
        input_output_aliases=aliases,
        compiler_params=pltpu.CompilerParams(vmem_limit_bytes=12 * MIB),
        cost_estimate=cost("attention"),
        name="attention",
    )(*arrays)


def join_kernel(before, down, low, high, out):
    out[0] = before[...]
    out[1] = total(down[...], low[...], high[...])


REDUCE = ((2, "far", "flip_far"), (3, "below", "flip_below"), (1, "above", "flip_above"), (0, "own", "flip"))
PARTS = ("below", "flip_below", "above", "flip_above", "own", "flip")


def hidden_kernel(sample, swap, grads, w, *refs):
    outs = dict(zip(PARTS, refs[-len(PARTS) :], strict=True))
    ends = refs[-len(PARTS) - 1 - sample : -len(PARTS)]
    kv = grads.at[sample] if len(grads.shape) == 3 else grads
    rows = slice(sample * TILE, (sample + 1) * TILE)
    a, y, _, _, _ = place()
    keys = [kv[:, 2 * h * DH : (2 * h + 1) * DH] for h in range(HEADS_DEV)]
    vals = [kv[:, (2 * h + 1) * DH : (2 * h + 2) * DH] for h in range(HEADS_DEV)]
    g = [swap[sample, :TILE], jnp.concatenate(keys, axis=1), jnp.concatenate(vals, axis=1)]
    for d, same, flip in REDUCE:
        yj = (y + d) & 3
        part = None
        for c in range(3):
            wc = jnp.concatenate([w[c, a, yj], w[c, 1 - a, yj]], axis=0)
            term = dot(g[c], wc, 1, 1)
            part = term if part is None else part + term
        part = part.astype(BF)
        if d != 2:
            outs[same][rows] = part[:, :CH]
            outs[flip][rows] = part[:, CH:]
        elif sample == 0:
            ends[0][:TILE] = part[:, CH:]
            ends[0][TILE:] = part[:, :CH]
        else:
            ends[0][...] = part[:, CH:]
            ends[1][...] = part[:, :CH]


def hidden_parts(sample, swap, grads, w, before):
    ends = [(ROWS, CH)] if sample == 0 else [(TILE, CH)] * 2
    arrays = [swap, grads, w, *before]
    return call(
        functools.partial(hidden_kernel, sample),
        "hidden_parts",
        arrays,
        ends + [(ROWS, CH)] * len(PARTS),
        4,
        input_output_aliases={3 + n: len(ends) + n for n in range(len(before))},
    )


def far_kernel(below, above, got_below, got_above, below_out, above_out):
    below_out[:TILE] = total(below[:TILE], got_below[:TILE])
    below_out[TILE:] = below[TILE:]
    above_out[:TILE] = above[:TILE]
    above_out[TILE:] = total(above[TILE:], got_above[...])


def near_kernel(below, flip, flip_below, flip_above, first, second, below_out, flip_out):
    below_out[:TILE] = total(below[:TILE], flip_below[:TILE], first[TILE:])
    below_out[TILE:] = total(below[TILE:], flip_below[TILE:], second[...])
    flip_out[...] = total(flip[...], flip_above[...])


def sum_kernel(*refs):
    refs[-1][...] = total(*[r[...] for r in refs[:-1]])


def hidden_reduce(first, got_flip, got_same, parts, text):
    part = dict(zip(PARTS, parts, strict=True))
    both = [(ROWS, CH)] * 2
    sides = [part["flip_below"], part["flip_above"], first, got_flip]
    flip_below, flip_above = call(
        far_kernel, "hidden_far", sides, both, 4, input_output_aliases={0: 0, 1: 1}
    )
    got = [head_move(flip_below, 1, 0), head_move(flip_above, 0, 1)]
    sides = [part["below"], part["flip"], *got, first, got_same]
    below, flip = call(
        near_kernel, "hidden_near", sides, both, 4, input_output_aliases={0: 0, 1: 1}
    )
    got = [head_move(below, 0, 3), head_move(part["above"], 0, 1), head_move(flip, 1, 0)]
    return (call(sum_kernel, "hidden_sum", [part["own"], *got], both[:1], 4)[0], text)


RING = [(CH // 2, 3 * CH)] * 2 + [(CH, 3 * CH)] * 3


def ring_store(outs, n, cols, part):
    if n == 0:
        outs[0][:, cols] = part[: CH // 2]
        outs[1][:, cols] = part[CH // 2 :]
    else:
        outs[n + 1][:, cols] = part


def query_weight_kernel(x_own, x_twin, own, twin, keep0, keep1, *outs):
    _, _, z, _, _ = place()
    g = jnp.concatenate([r[s, :TILE] for r in (own, twin) for s in range(SAMPLES)], axis=0)
    for s, keep in enumerate((keep0, keep1)):
        outs[5][s] = total(keep[...], twin[s, TILE:])
    for n, d in enumerate((2, 1, 3, 0)):
        j = (z + d) & 3
        x = jnp.concatenate([x_own[j], x_twin[j]], axis=0)
        ring_store(outs, n, slice(0, CH), dot(x, g, 0, 0).astype(BF))


def query_weight_parts(*arrays):
    shapes = [*RING, (SAMPLES, TEXT, CH)]
    return call(query_weight_kernel, "query_weight_parts", arrays, shapes, 4)


def weight_kernel(x_own, x_twin, own, twin, *refs):
    outs = refs[len(RING) :]
    _, _, z, _, _ = place()
    g = jnp.concatenate([r[s] for r in (own, twin) for s in range(SAMPLES)], axis=0)
    for n, d in enumerate((2, 1, 3, 0)):
        j = (z + d) & 3
        x = jnp.concatenate([x_own[j], x_twin[j]], axis=0)
        part = dot(x, g, 0, 0).astype(BF)
        for h in range(HEADS_DEV):
            for k in range(2):
                at, to = ((2 * h + k) * DH, (k + 1) * CH + h * DH)
                ring_store(outs, n, slice(to, to + DH), part[:, at : at + DH])


def weight_parts(arrays, before):
    aliases = {len(arrays) + n: n for n in range(len(RING))}
    arrays = [*arrays, *before]
    return call(weight_kernel, "weight_parts", arrays, RING, 6, input_output_aliases=aliases)


def weight_far_kernel(up, down, got_up, got_down, up_out, down_out):
    half = CH // 2
    up_out[:half] = total(up[:half], got_up[...])
    up_out[half:] = up[half:]
    down_out[:half] = down[:half]
    down_out[half:] = total(down[half:], got_down[...])


def weight_ring(text, far_up, far_down, up, down, own):
    got = [slab_move(far_up, 1, 0, 0), slab_move(far_down, 3, 0, 0)]
    got, text = lax.optimization_barrier((got, text))
    both = RING[3:]
    up, down = call(
        weight_far_kernel, "weight_far", [up, down, *got], both, 4, input_output_aliases={0: 0, 1: 1}
    )
    return ([own, slab_move(up, 1, 0, 0), slab_move(down, 3, 0, 0)], text)


def weight_halves_kernel(own, up, down, near, far):
    _, _, _, x, core = place()
    home = x == core
    for half in range(2):
        rows = slice(half * CH // 2, (half + 1) * CH // 2)
        part = total(own[rows], up[rows], down[rows])
        is_far = (core == half) == home

        @pl.when(is_far)
        def _():
            far[...] = part

        @pl.when(jnp.logical_not(is_far))
        def _():
            near[...] = part


def weight_final_kernel(far, got_first, got_second, out):
    _, _, _, x, core = place()
    for c in range(3):
        cols = slice(c * CH, (c + 1) * CH)
        kept = jnp.where(x == core, far[:, cols], got_second[:, cols])
        out[c] = total(kept, got_first[:, cols])


def weight_home(parts):
    half = (CH // 2, 3 * CH)
    near, far = call(weight_halves_kernel, "weight_halves", parts, [half, half], 6)
    first, second = ([], [])
    for s in range(16):
        z, x, c = (s // 4, s // 2 % 2, s % 2)
        if x == c:
            first.append((s, z * 4 + x * 2 + 1 - c))
        else:
            first.append((s, z * 4 + (1 - x) * 2 + c))
            second.append((s, z * 4 + (1 - x) * 2 + 1 - c))
    got_first = lax.ppermute(near, "slab", first)
    got_second = lax.ppermute(far, "slab", second)
    out = call(
        weight_final_kernel, "weight_final", [far, got_first, got_second], [(3, CH // 2, CH)], 4
    )[0]
    return jnp.transpose(out, (1, 0, 2))


def text_final_kernel(full, twin, key, value):
    _, _, _, _, core = place()
    key[...] = jnp.where(core == 0, full[...], twin[...])
    value[...] = jnp.where(core == 0, twin[...], full[...])


def text_step(part, bit):
    got = lax.ppermute(part, "slab", [(s, s ^ bit) for s in range(16)])
    return call(sum_kernel, "text_pair", [part, got], [part.shape], 4)[0]


def text_final(part):
    both = [part, slab_move(part, 0, 0, 1)]
    return jnp.stack(call(text_final_kernel, "text_final", both, [part.shape] * 2, 4), axis=2)


def body(hidden, w_qkv, text_keys, text_values, text_len, advantage, out_grad, tile_lists):
    w = jnp.transpose(w_qkv, (1, 0, 2)).reshape(3, 2, 4, CH, CH)
    scalars = (tile_lists, text_len, advantage)
    w, q, *kvs, mine, other = project(hidden, w)
    halos = [(slab_step(kvs[0], 1), slab_step(kvs[0], -1))]
    late = kvs[1]
    halos, other = lax.optimization_barrier((halos, other))
    theirs = slab_move(other, 0, 0, 1)
    halos.append((slab_step(late, 1), slab_step(late, -1)))
    ends, keeps, swap = ([], [], None)
    for s in range(SAMPLES):
        if s == 1:
            q, _, theirs = lax.optimization_barrier((q, swap, theirs))
        swap, dprev, down, dnext, keep = attention(
            s, scalars, q, halos[s][0], kvs[s], halos[s][1], text_keys, text_values, out_grad, swap
        )
        keeps.append(keep)
        ends.append((down, dnext, dprev))
    sums = [(ends[0][0], slab_step(ends[0][1], 1), slab_step(ends[0][2], -1))]
    down, dnext, dprev = ends[1]
    sums, swap, dnext, dprev = lax.optimization_barrier((sums, swap, dnext, dprev))
    sums.append((down, slab_step(dnext, 1), slab_step(dprev, -1)))
    swap_twin = slab_move(swap, 0, 0, 1)
    *query, text = query_weight_parts(mine, theirs, swap, swap_twin, *keeps)
    grad, _ = lax.optimization_barrier((total(*sums[0]), text))
    first, *parts = hidden_parts(0, swap, grad, w, [])
    first = head_move(first, 0, 3)
    text = text_step(text, 4)
    sums[1], _, text = lax.optimization_barrier((sums[1], parts, text))
    grads = call(join_kernel, "join", [grad, *sums[1]], [(SAMPLES, TILE, 2 * CH)], 4)[0]
    twin = slab_move(grads, 0, 0, 1)
    last_flip, last_same, *parts = hidden_parts(1, swap, grads, w, parts)
    last = (head_move(last_flip, 0, 1), head_move(last_same, 0, 3))
    text = text_step(text, 8)
    twin, _, text = lax.optimization_barrier((twin, last_flip, text))
    rest = weight_parts([mine, theirs, grads, twin], query)
    hidden_grad, text = hidden_reduce(first, *last, parts, text)
    text = text_step(text, 2)
    ring, text = weight_ring(text, *rest)
    text_grad = text_final(text)
    weight_grad = weight_home(ring)
    return (hidden_grad, weight_grad, text_grad)


def solution(mesh):
    in_specs = (
        P("slab", "head"),
        P(None, None, "head"),
        P(None, None, "head"),
        P(None, None, "head"),
        P(),
        P(),
        P("slab", "head"),
        P("slab", None),
    )
    out_specs = (P("slab", "head"), P("slab", None, "head"), P(None, None, None, "head"))
    return jax.shard_map(body, mesh=mesh, in_specs=in_specs, out_specs=out_specs, check_vma=False)
```
